32 devices in a mesh: blk: 8 (over z, y), dp: 4 (over x, core).
Axes of the slice: x: 2, y: 2, z: 4, core: 2. Of those that a mesh axis runs over, the one named last changes fastest.
Arguments:
- frames: bfloat16 [131072, 768], P(('blk', 'dp')), may hold values from -6 to 6
- lengths: int32 [4096], P(('blk', 'dp')), may hold values from 1 to 32, as said below
- routes: int32 [32, 4, 512], P(('blk', 'dp')), may hold values from -1 to 2047, as said below
- w_first: bfloat16 [768, 512], replicated, may hold values from -0.21875 to 0.21875
- b_first: float32 [512], replicated, may hold values from -3 to 3
- w_second: bfloat16 [512, 512], replicated, may hold values from -0.25 to 0.25
- captions: bfloat16 [4096, 512], P(('blk', 'dp')), may hold values from -6 to 6
- logit_scale: float32 [], replicated, may hold values from 10 to 30
Outputs:
- grad_pooled: float32 [4096, 512], P(('blk', 'dp'))
- grad_text: float32 [4096, 512], P(('blk', 'dp'))
The draws below stay inside these ranges and needn't reach their ends.
Inputs may be any that keep to these rules, and one draw needn't show every extreme that they name: Each device has at most 2048 live frame rows (the sum of its clips' lengths), and exactly 2048 on some device. `routes`: every live frame row of a device appears exactly once in its table and no other row appears; each owner's slots are filled from the front; on some device every slot is filled.
All inputs are finite; a program needn't handle non-finite values.
Results may differ from the reference program's by a relative error of at most 0.0061.
Values may be sent and summed in bfloat16 or wider, within the bound.
No kernel may reach another device: no remote copies, remote signals or barrier semaphores. Data moves between devices by JAX's collectives and lax.ppermute only.
A program may use at most 64 MiB of HBM per device.

```python
import jax
import jax.numpy as jnp
from jax import lax

D_FRAME = 768
EMB = 512
CLIPS_DEV = 128
MAXF = 32
FRAMES_DEV = 4096
PAIRS = 4096
FRAME_ROWS = 131072
N_BLK = 8
N_DP = 4


def frame_plan(key):
    devices = N_BLK * N_DP
    upper = jax.random.randint(jax.random.fold_in(key, 11), (devices, 1), 8, 16)
    clip_lengths = jax.random.randint(jax.random.fold_in(key, 12), (devices, CLIPS_DEV), 1, upper + 1)
    clip_lengths = clip_lengths.at[:, 0].set(MAXF)
    full_device = jax.random.randint(jax.random.fold_in(key, 13), (), 0, devices)
    device_iota = jnp.arange(devices, dtype=jnp.int32)
    clip_lengths = jnp.where(device_iota[:, None] == full_device, MAXF // 2, clip_lengths).astype(jnp.int32)
    totals = jnp.sum(clip_lengths, axis=1)
    rotation = jax.random.randint(jax.random.fold_in(key, 14), (devices,), 0, N_DP)
    slot_count = CLIPS_DEV * MAXF // 2 // N_DP
    owner_iota = jnp.arange(N_DP, dtype=jnp.int32)
    slot_iota = jnp.arange(slot_count, dtype=jnp.int32)
    local_rows = slot_iota[None, None, :] * N_DP + jnp.mod(owner_iota[None, :, None] - rotation[:, None, None], N_DP)
    route_table = jnp.where(local_rows < totals[:, None, None], local_rows, -1).astype(jnp.int32)
    return (clip_lengths.reshape(-1), route_table)


def draw_lengths(key, part):
    return frame_plan(key)[0]


def draw_routes(key, part):
    return frame_plan(key)[1]


def block_levels(rng, extent, cuts, low, largest):
    loudness, own = 1.0, jax.random.fold_in(rng, 6)
    for position, blocks in cuts:
        heights = jnp.exp(jax.random.uniform(jax.random.fold_in(own, position), (blocks,), jnp.float32, low / len(cuts), largest / len(cuts)))
        loudness = loudness * jnp.repeat(heights, extent[position] // blocks).reshape([-1 if axis == position else 1 for axis in range(len(extent))])
    return loudness


def bell_draw(own_key, shape, scale, bound, cuts=(), kind=jnp.bfloat16):
    factor_of = block_levels(own_key, shape, cuts, -0.22, 0.18) if cuts else 1.0
    drawn = jax.random.normal(own_key, shape, jnp.float32) * scale * factor_of
    return jnp.minimum(jnp.maximum(drawn, -bound), bound).astype(kind)


def setup_inputs(seed: int = 0) -> dict:
    keys = jax.random.split(jax.random.key(seed), 9)
    return {
        "frames": bell_draw(keys[0], (FRAME_ROWS, D_FRAME), 1.0, 6.0, ((0, 32),)),
        "lengths": draw_lengths(jax.random.fold_in(keys[8], 71), 0),
        "routes": draw_routes(jax.random.fold_in(keys[8], 71), 0),
        "w_first": bell_draw(keys[3], (D_FRAME, EMB), D_FRAME ** -0.5, 0.21875),
        "b_first": bell_draw(keys[4], (EMB,), 0.5, 3.0, (), jnp.float32),
        "w_second": bell_draw(keys[5], (EMB, EMB), EMB ** -0.5, 0.25),
        "captions": bell_draw(keys[6], (PAIRS, EMB), 1.0, 6.0, ((0, 32),)),
        "logit_scale": jnp.clip(jax.random.uniform(keys[7], (), jnp.float32, 10.0, 30.0), 10.0, 30.0),
    }


epsilon = 1e-06

def frame_project(frame_rows, w_first, b_first, w_second):
    before = jnp.dot(frame_rows, w_first, preferred_element_type=jnp.float32) + b_first
    active = jax.nn.gelu(before).astype(jnp.bfloat16)
    return jnp.dot(active, w_second, preferred_element_type=jnp.float32).astype(jnp.bfloat16)

def clip_of_rows(lengths_dev, row_count):
    clip_ends = jnp.cumsum(lengths_dev)
    positions = jnp.arange(row_count, dtype=jnp.int32)
    return lax.optimization_barrier(jnp.sum((clip_ends[None, :] <= positions[:, None]).astype(jnp.int32), axis=1)).astype(jnp.int32)

def unit_rows(values):
    radius = jnp.sqrt(lax.optimization_barrier(jnp.sum(values * values, axis=-1, keepdims=True)) + epsilon)
    return (values / radius, radius)

def unit_backward(unit_vec, radius, upstream):
    return (upstream - unit_vec * lax.optimization_barrier(jnp.sum(unit_vec * upstream, axis=-1, keepdims=True))) / radius

def reference(frames, lengths, routes, w_first, b_first, w_second, captions, logit_scale):
    devices = N_BLK * N_DP
    frame_blocks = frames.reshape(devices, FRAMES_DEV, D_FRAME)
    length_blocks = lengths.reshape(devices, CLIPS_DEV)
    clip_iota = jnp.arange(CLIPS_DEV, dtype=jnp.int32)

    def device_sums(inputs):
        frames_dev, lengths_dev, routes_dev = inputs
        clip_ids = clip_of_rows(lengths_dev, FRAMES_DEV)
        is_live = (routes_dev >= 0).reshape(-1)
        safe_rows = jnp.where(is_live, routes_dev.reshape(-1), 0).astype(jnp.int32)
        hidden = frame_project(frames_dev[safe_rows], w_first, b_first, w_second)
        slot_clips = jnp.where(is_live, clip_ids[safe_rows], -1)
        onehot = (slot_clips[:, None] == clip_iota[None, :]).astype(jnp.bfloat16)
        return jnp.dot(onehot.T, hidden, preferred_element_type=jnp.float32)
    pooled_sums = lax.map(device_sums, (frame_blocks, length_blocks, routes)).reshape(PAIRS, EMB)
    pooled = pooled_sums / lengths.astype(jnp.float32)[:, None]
    audio_unit, audio_radius = unit_rows(pooled)
    text_unit, text_radius = unit_rows(captions.astype(jnp.float32))
    audio_low = audio_unit.astype(jnp.bfloat16)
    text_low = text_unit.astype(jnp.bfloat16)

    def regroup(values):
        return values.reshape(N_BLK, N_DP, CLIPS_DEV, EMB).transpose(1, 0, 2, 3).reshape(N_DP, N_BLK * CLIPS_DEV, EMB)

    def ungroup(values):
        return values.reshape(N_DP, N_BLK, CLIPS_DEV, EMB).transpose(1, 0, 2, 3).reshape(PAIRS, EMB)
    identity = jnp.eye(N_BLK * CLIPS_DEV, dtype=jnp.float32)

    def group_terms(inputs):
        audio_group, text_group = inputs
        logits = logit_scale * jnp.dot(audio_group, text_group.T, preferred_element_type=jnp.float32)
        row_lse = jax.nn.logsumexp(logits, axis=1)
        col_lse = jax.nn.logsumexp(logits, axis=0)
        weights = ((jnp.exp(logits - row_lse[:, None]) + jnp.exp(logits - col_lse[None, :]) - 2.0 * identity) / (2.0 * PAIRS)).astype(jnp.bfloat16)
        grad_audio = logit_scale * jnp.dot(weights, text_group, preferred_element_type=jnp.float32)
        grad_caption = logit_scale * jnp.dot(weights.T, audio_group, preferred_element_type=jnp.float32)
        return (grad_audio, grad_caption)
    grad_audio, grad_caption = lax.map(group_terms, (regroup(audio_low), regroup(text_low)))
    grad_pooled = unit_backward(audio_unit, audio_radius, ungroup(grad_audio))
    grad_text = unit_backward(text_unit, text_radius, ungroup(grad_caption))
    return (grad_pooled, grad_text)
```

```python
import functools
import math

import jax
import jax.numpy as jnp
from jax import lax
from jax.experimental import pallas as pl
from jax.experimental.pallas import tpu as pltpu
from jax.sharding import PartitionSpec as P

epsilon = 1e-06
LOG2E = math.log2(math.e)
F32 = jnp.float32
BF16 = jnp.bfloat16
VMEM = pl.BlockSpec(memory_space=pltpu.VMEM)
SMEM = pl.BlockSpec(memory_space=pltpu.SMEM)
HBM = pl.BlockSpec(memory_space=pl.ANY)
PARAMS = pltpu.CompilerParams(vmem_limit_bytes=40 * 1024 * 1024)


def mm(left, right, left_dim=1, right_dim=0):
    return lax.dot_general(
        left, right, (((left_dim,), (right_dim,)), ((), ())), preferred_element_type=F32
    )


def swap(block, offset):
    count = lax.axis_size("blk")
    return lax.ppermute(block, "blk", [(i ^ offset, i) for i in range(count)])


def text_kernel(captions_ref, low_ref):
    values = captions_ref[...].astype(F32)
    radius = jnp.sqrt(jnp.sum(values * values, axis=1, keepdims=True) + epsilon)
    low_ref[...] = (values / radius).astype(BF16)


def frames_kernel(
    rows, step, lengths_ref, bias_ref, first_ref, second_ref, frames_ref, pooled_ref, low_ref, held, sems
):
    steps = rows // step
    copies = [
        pltpu.make_async_copy(
            frames_ref.at[pl.ds(k * step, step)], held.at[pl.ds(k * step, step)], sems.at[k]
        )
        for k in range(steps)
    ]
    for copy in copies:
        copy.start()
    clips = lengths_ref.shape[1]
    lengths = lengths_ref[...].astype(F32)
    row_id = lax.broadcasted_iota(jnp.int32, (clips, clips), 0)
    col_id = lax.broadcasted_iota(jnp.int32, (clips, clips), 1)
    ends = jnp.sum(jnp.where(col_id <= row_id, lengths, 0.0), axis=1, keepdims=True)
    sizes = jnp.sum(jnp.where(col_id == row_id, lengths, 0.0), axis=1, keepdims=True)
    starts = ends - sizes
    bias = bias_ref[...]
    first = first_ref[...]
    slot = lax.broadcasted_iota(jnp.int32, (clips, step), 1).astype(F32)
    total = jnp.zeros(pooled_ref.shape, F32)
    root = math.sqrt(2.0 / math.pi)
    for k in range(steps):
        copies[k].wait()
        before = mm(held[pl.ds(k * step, step), :], first) + bias
        half = before * 0.5
        inner = before * (root + (root * 0.044715) * (before * before))
        active = (half + half * jnp.tanh(inner)).astype(BF16)
        place = slot + float(k * step)
        onehot = jnp.where((place >= starts) & (place < ends), 1.0, 0.0).astype(BF16)
        total = total + mm(onehot, active)
    high = total.astype(BF16)
    rest = (total - high.astype(F32)).astype(BF16)
    second = second_ref[...]
    pooled = (mm(high, second) + mm(rest, second)) / sizes
    pooled_ref[...] = pooled
    radius = jnp.sqrt(jnp.sum(pooled * pooled, axis=1, keepdims=True) + epsilon)
    low_ref[...] = (pooled / radius).astype(BF16)


def tile_kernel(row_blocks, col_blocks, scale_ref, *refs):
    audio = refs[:row_blocks]
    text = refs[row_blocks : row_blocks + col_blocks]
    grown_ref, row_ref, col_ref = refs[row_blocks + col_blocks :]
    block = audio[0].shape[0]
    factor = scale_ref[0, 0] * LOG2E
    col_sums = [None] * col_blocks
    for r in range(row_blocks):
        rows = audio[r][...]
        partial = None
        for c in range(col_blocks):
            grown = jnp.exp2(mm(rows, text[c][...], 1, 1) * factor)
            grown_ref[pl.ds(r * block, block), pl.ds(c * block, block)] = grown
            down = jnp.sum(grown, axis=0, keepdims=True)
            col_sums[c] = down if r == 0 else col_sums[c] + down
            partial = grown if c == 0 else partial + grown
        row_ref[pl.ds(r, 1), :] = jnp.sum(partial.T, axis=0, keepdims=True)
    for c in range(col_blocks):
        col_ref[pl.ds(c, 1), :] = col_sums[c]


def grad_kernel(row_blocks, col_blocks, *refs):
    refs = list(refs)
    grown_ref, row_ref, col_ref = refs[:3]
    others_row = refs[3 : 3 + row_blocks - 1]
    others_col = refs[2 + row_blocks : 2 + row_blocks + col_blocks - 1]
    at = 1 + row_blocks + col_blocks
    audio = refs[at : at + row_blocks]
    text = refs[at + row_blocks : at + row_blocks + col_blocks]
    outs = refs[at + row_blocks + col_blocks :]
    audio_outs, text_outs = outs[:row_blocks], outs[row_blocks:]
    block = audio[0].shape[0]
    row_inverse = []
    for r in range(row_blocks):
        total = row_ref[pl.ds(r, 1), :]
        for m in range(1, row_blocks):
            total = total + others_row[m - 1][pl.ds(m ^ r, 1), :]
        spread = jnp.broadcast_to(1.0 / total, (block, block))
        row_inverse.append(spread.T)
    col_inverse = []
    for c in range(col_blocks):
        total = col_ref[pl.ds(c, 1), :]
        for m in range(1, col_blocks):
            total = total + others_col[m - 1][pl.ds(m ^ c, 1), :]
        col_inverse.append(1.0 / total)
    weights = [
        [
            (
                grown_ref[pl.ds(r * block, block), pl.ds(c * block, block)]
                * (row_inverse[r] + col_inverse[c])
            ).astype(BF16)
            for c in range(col_blocks)
        ]
        for r in range(row_blocks)
    ]
    for r in reversed(range(row_blocks)):
        total = sum(mm(weights[r][c], text[c][...]) for c in range(col_blocks))
        audio_outs[r][...] = total.astype(audio_outs[r].dtype)
    for c in reversed(range(col_blocks)):
        total = sum(mm(weights[r][c], audio[r][...], 0, 0) for r in range(row_blocks))
        text_outs[c][...] = total.astype(text_outs[c].dtype)


def final_kernel(row_blocks, col_blocks, pair_count, scale_ref, *refs):
    pooled_ref, captions_ref, audio_ref, text_ref = refs[:4]
    audio_parts = refs[4 : 4 + row_blocks]
    text_parts = refs[4 + row_blocks : 4 + row_blocks + col_blocks]
    audio_out, text_out = refs[4 + row_blocks + col_blocks :]
    factor = scale_ref[0, 0] / (2.0 * pair_count)

    def back(values, parts, partner, out):
        total = parts[0][...] - 2.0 * partner.astype(F32)
        for part in parts[1:]:
            total = total + part[...].astype(F32)
        total = total * factor
        radius = jnp.sqrt(jnp.sum(values * values, axis=1, keepdims=True) + epsilon)
        inverse = 1.0 / radius
        unit = values * inverse
        along = jnp.sum(unit * total, axis=1, keepdims=True)
        out[...] = (total - unit * along) * inverse

    back(pooled_ref[...], audio_parts, text_ref[...], audio_out)
    back(captions_ref[...].astype(F32), text_parts, audio_ref[...], text_out)


def local(frames, lengths, routes, w_first, b_first, w_second, captions, logit_scale):
    clips = lengths.shape[0]
    width = w_second.shape[1]
    group = lax.axis_size("blk")
    pair_count = clips * group * lax.axis_size("dp")
    col_blocks = min(4, group)
    row_blocks = group // col_blocks
    live_rows = min(routes.shape[1] * routes.shape[2], frames.shape[0])
    step = min(256, live_rows)
    scale = logit_scale.reshape(1, 1)
    block_low = jax.ShapeDtypeStruct((clips, width), BF16)
    block_full = jax.ShapeDtypeStruct((clips, width), F32)

    text_low = pl.pallas_call(
        text_kernel, out_shape=block_low, in_specs=[VMEM], out_specs=VMEM, compiler_params=PARAMS
    )(captions)
    text = [text_low] + [swap(text_low, c) for c in range(1, col_blocks)]
    pooled, audio_low = pl.pallas_call(
        functools.partial(frames_kernel, live_rows, step),
        out_shape=(block_full, block_low),
        in_specs=[VMEM] * 4 + [HBM],
        out_specs=(VMEM, VMEM),
        scratch_shapes=[
            pltpu.VMEM((live_rows, frames.shape[1]), BF16),
            pltpu.SemaphoreType.DMA((live_rows // step,)),
        ],
        compiler_params=PARAMS,
    )(lengths.reshape(1, clips), b_first.reshape(1, -1), w_first, w_second, frames)
    audio = [audio_low] + [swap(audio_low, col_blocks * r) for r in range(1, row_blocks)]
    grown, row_sum, col_sum = pl.pallas_call(
        functools.partial(tile_kernel, row_blocks, col_blocks),
        out_shape=(
            jax.ShapeDtypeStruct((row_blocks * clips, col_blocks * clips), F32),
            jax.ShapeDtypeStruct((row_blocks, clips), F32),
            jax.ShapeDtypeStruct((col_blocks, clips), F32),
        ),
        in_specs=[SMEM] + [VMEM] * (row_blocks + col_blocks),
        out_specs=(VMEM, VMEM, VMEM),
        compiler_params=PARAMS,
    )(scale, *audio, *text)
    row_others = [swap(row_sum, col_blocks * r) for r in range(1, row_blocks)]
    col_others = [swap(col_sum, c) for c in range(1, col_blocks)]
    parts = pl.pallas_call(
        functools.partial(grad_kernel, row_blocks, col_blocks),
        out_shape=[block_full if r == 0 else block_low for r in range(row_blocks)]
        + [block_full if c == 0 else block_low for c in range(col_blocks)],
        in_specs=[VMEM] * (1 + 2 * (row_blocks + col_blocks)),
        out_specs=[VMEM] * (row_blocks + col_blocks),
        compiler_params=PARAMS,
    )(grown, row_sum, col_sum, *row_others, *col_others, *audio, *text)
    audio_parts = [parts[0]] + [swap(parts[r], col_blocks * r) for r in range(1, row_blocks)]
    text_parts = [parts[row_blocks]] + [
        swap(parts[row_blocks + c], c) for c in range(1, col_blocks)
    ]
    return pl.pallas_call(
        functools.partial(final_kernel, row_blocks, col_blocks, pair_count),
        out_shape=(block_full, block_full),
        in_specs=[SMEM] + [VMEM] * (4 + row_blocks + col_blocks),
        out_specs=(VMEM, VMEM),
        compiler_params=PARAMS,
    )(scale, pooled, captions, audio_low, text_low, *audio_parts, *text_parts)


def solution(mesh):
    rows = P(("blk", "dp"))
    return jax.shard_map(
        local,
        mesh=mesh,
        in_specs=(rows, rows, rows, P(), P(), P(), rows, P()),
        out_specs=(rows, rows),
        check_vma=False,
    )
```

```python
import functools
import math

import jax
import jax.numpy as jnp
from jax import lax
from jax.experimental import pallas as pl
from jax.experimental.pallas import tpu as pltpu
from jax.sharding import PartitionSpec as P

epsilon = 1e-06
LOG2E = math.log2(math.e)
F32 = jnp.float32
BF16 = jnp.bfloat16
VMEM = pl.BlockSpec(memory_space=pltpu.VMEM)
SMEM = pl.BlockSpec(memory_space=pltpu.SMEM)
HBM = pl.BlockSpec(memory_space=pltpu.HBM)
PARAMS = pltpu.CompilerParams(vmem_limit_bytes=40 * 1024 * 1024)


def mm(left, right, left_dim=1, right_dim=0):
    return lax.dot_general(
        left, right, (((left_dim,), (right_dim,)), ((), ())), preferred_element_type=F32
    )


def in_hbm(array):
    return pltpu.with_memory_space_constraint(array, pltpu.HBM)


def swap(block, offset):
    count = lax.axis_size("blk")
    return lax.ppermute(block, "blk", [(i ^ offset, i) for i in range(count)])


def unit_low(values):
    return values * lax.rsqrt(jnp.sum(values * values, axis=1, keepdims=True) + epsilon)


def frames_kernel(chunks, *refs):
    lengths_hbm, bias_hbm, first_hbm, second_hbm, captions_hbm, frames_hbm = refs[:6]
    pooled_ref, audio_ref, text_ref = refs[6:9]
    lengths_ref, bias_ref, first_ref, second_ref, captions_ref, held, sems = refs[9:]
    copies = []
    at = 0
    for k, rows in enumerate(chunks):
        part = pl.ds(at, rows)
        copies.append(pltpu.make_async_copy(frames_hbm.at[part], held.at[part], sems.at[k]))
        at += rows
    extra = []
    for k, pair in enumerate(
        [
            (first_hbm, first_ref),
            (lengths_hbm, lengths_ref),
            (bias_hbm, bias_ref),
            (captions_hbm, captions_ref),
            (second_hbm, second_ref),
        ]
    ):
        extra.append(pltpu.make_async_copy(*pair, sems.at[len(chunks) + k]))
    first_copy, lengths_copy, bias_copy, captions_copy, second_copy = extra
    for copy in [lengths_copy, first_copy, copies[0], captions_copy, bias_copy, *copies[1:], second_copy]:
        copy.start()
    clips = lengths_ref.shape[1]
    lengths_copy.wait()
    lengths = lengths_ref[...].astype(F32)
    row_id = lax.broadcasted_iota(jnp.int32, (clips, clips), 0)
    col_id = lax.broadcasted_iota(jnp.int32, (clips, clips), 1)
    ends = jnp.sum(jnp.where(col_id <= row_id, lengths, 0.0), axis=1, keepdims=True)
    sizes = jnp.sum(jnp.where(col_id == row_id, lengths, 0.0), axis=1, keepdims=True)
    starts = ends - sizes
    live = jnp.sum(lengths_ref[...])
    captions_copy.wait()
    text_ref[...] = unit_low(captions_ref[...].astype(F32)).astype(BF16)
    bias_copy.wait()
    first_copy.wait()
    root = math.sqrt(2.0 / math.pi)

    def pooled_chunk(at, rows):
        before = mm(held[pl.ds(at, rows), :], first_ref[...]) + bias_ref[...]
        half = before * 0.5
        inner = before * (root + (root * 0.044715) * (before * before))
        active = (half + half * jnp.tanh(inner)).astype(BF16)
        place = lax.broadcasted_iota(jnp.int32, (clips, rows), 1).astype(F32) + float(at)
        onehot = jnp.where((place >= starts) & (place < ends), 1.0, 0.0).astype(BF16)
        return mm(onehot, active)

    at = 0
    for k, rows in enumerate(chunks):
        copies[k].wait()
        if k == 0:
            pooled_ref[...] = pooled_chunk(at, rows)
        else:

            @pl.when(live > at)
            def _():
                pooled_ref[...] += pooled_chunk(at, rows)

        at += rows
    second_copy.wait()
    total = pooled_ref[...]
    high = total.astype(BF16)
    rest = (total - high.astype(F32)).astype(BF16)
    second = second_ref[...]
    pooled = (mm(high, second) + mm(rest, second)) / sizes
    pooled_ref[...] = pooled
    audio_ref[...] = unit_low(pooled).astype(BF16)


def tile_kernel(row_blocks, col_blocks, scale_ref, *refs):
    audio = refs[:row_blocks]
    text = refs[row_blocks : row_blocks + col_blocks]
    grown_ref, row_ref, col_ref = refs[row_blocks + col_blocks :]
    block = audio[0].shape[0]
    factor = scale_ref[0, 0] * LOG2E
    col_sums = [None] * col_blocks
    for r in range(row_blocks):
        rows = audio[r][...]
        partial = None
        for c in range(col_blocks):
            grown = jnp.exp2(mm(rows, text[c][...], 1, 1) * factor)
            grown_ref[pl.ds(r * block, block), pl.ds(c * block, block)] = grown
            down = jnp.sum(grown, axis=0, keepdims=True)
            col_sums[c] = down if r == 0 else col_sums[c] + down
            partial = grown if c == 0 else partial + grown
        row_ref[pl.ds(r, 1), :] = jnp.sum(partial.T, axis=0, keepdims=True)
    for c in range(col_blocks):
        col_ref[pl.ds(c, 1), :] = col_sums[c]


def grad_kernel(row_blocks, col_blocks, *refs):
    refs = list(refs)
    grown_ref, row_ref, col_ref = refs[:3]
    others_row = refs[3 : 3 + row_blocks - 1]
    others_col = refs[2 + row_blocks : 2 + row_blocks + col_blocks - 1]
    at = 1 + row_blocks + col_blocks
    audio = refs[at : at + row_blocks]
    text = refs[at + row_blocks : at + row_blocks + col_blocks]
    outs = refs[at + row_blocks + col_blocks :]
    audio_outs, text_outs = outs[:row_blocks], outs[row_blocks:]
    block = audio[0].shape[0]
    row_inverse = []
    for r in range(row_blocks):
        total = row_ref[pl.ds(r, 1), :]
        for m in range(1, row_blocks):
            total = total + others_row[m - 1][pl.ds(m ^ r, 1), :]
        spread = jnp.broadcast_to(1.0 / total, (block, block))
        row_inverse.append(spread.T)
    col_inverse = []
    for c in range(col_blocks):
        total = col_ref[pl.ds(c, 1), :]
        for m in range(1, col_blocks):
            total = total + others_col[m - 1][pl.ds(m ^ c, 1), :]
        col_inverse.append(1.0 / total)
    weights = [
        [
            (
                grown_ref[pl.ds(r * block, block), pl.ds(c * block, block)]
                * (row_inverse[r] + col_inverse[c])
            ).astype(BF16)
            for c in range(col_blocks)
        ]
        for r in range(row_blocks)
    ]
    for r in reversed(range(row_blocks)):
        total = sum(mm(weights[r][c], text[c][...]) for c in range(col_blocks))
        audio_outs[r][...] = total.astype(audio_outs[r].dtype)
    for c in reversed(range(col_blocks)):
        total = sum(mm(weights[r][c], audio[r][...], 0, 0) for r in range(row_blocks))
        text_outs[c][...] = total.astype(text_outs[c].dtype)


def final_kernel(row_blocks, col_blocks, pair_count, scale_ref, *refs):
    pooled_ref, captions_ref, audio_ref, text_ref = refs[:4]
    audio_parts = refs[4 : 4 + row_blocks]
    text_parts = refs[4 + row_blocks : 4 + row_blocks + col_blocks]
    audio_out, text_out = refs[4 + row_blocks + col_blocks :]
    factor = scale_ref[0, 0] / (2.0 * pair_count)

    def back(values, parts, partner, out):
        total = parts[0][...] - 2.0 * partner.astype(F32)
        for part in parts[1:]:
            total = total + part[...].astype(F32)
        total = total * factor
        radius = jnp.sqrt(jnp.sum(values * values, axis=1, keepdims=True) + epsilon)
        inverse = 1.0 / radius
        unit = values * inverse
        along = jnp.sum(unit * total, axis=1, keepdims=True)
        out[...] = (total - unit * along) * inverse

    back(pooled_ref[...], audio_parts, text_ref[...], audio_out)
    back(captions_ref[...].astype(F32), text_parts, audio_ref[...], text_out)


def local(frames, lengths, routes, w_first, b_first, w_second, captions, logit_scale):
    clips = lengths.shape[0]
    width = w_second.shape[1]
    group = lax.axis_size("blk")
    pair_count = clips * group * lax.axis_size("dp")
    col_blocks = min(4, group)
    row_blocks = group // col_blocks
    live_rows = min(routes.shape[1] * routes.shape[2], frames.shape[0])
    chunks = [live_rows // 2, live_rows // 4]
    chunks.append(live_rows - sum(chunks))
    scale = logit_scale.reshape(1, 1)
    block_low = jax.ShapeDtypeStruct((clips, width), BF16)
    block_full = jax.ShapeDtypeStruct((clips, width), F32)

    pooled, audio_low, text_low = pl.pallas_call(
        functools.partial(frames_kernel, chunks),
        out_shape=(block_full, block_low, block_low),
        in_specs=[HBM] * 6,
        out_specs=(VMEM, VMEM, VMEM),
        scratch_shapes=[
            pltpu.VMEM((1, clips), lengths.dtype),
            pltpu.VMEM((1, width), F32),
            pltpu.VMEM(w_first.shape, BF16),
            pltpu.VMEM(w_second.shape, BF16),
            pltpu.VMEM((clips, width), BF16),
            pltpu.VMEM((live_rows, frames.shape[1]), BF16),
            pltpu.SemaphoreType.DMA((len(chunks) + 5,)),
        ],
        compiler_params=PARAMS,
    )(
        *map(
            in_hbm,
            (lengths.reshape(1, clips), b_first.reshape(1, width), w_first, w_second, captions, frames),
        )
    )
    text = [text_low] + [swap(text_low, c) for c in range(1, col_blocks)]
    audio = [audio_low] + [swap(audio_low, col_blocks * r) for r in range(1, row_blocks)]
    grown, row_sum, col_sum = pl.pallas_call(
        functools.partial(tile_kernel, row_blocks, col_blocks),
        out_shape=(
            jax.ShapeDtypeStruct((row_blocks * clips, col_blocks * clips), F32),
            jax.ShapeDtypeStruct((row_blocks, clips), F32),
            jax.ShapeDtypeStruct((col_blocks, clips), F32),
        ),
        in_specs=[SMEM] + [VMEM] * (row_blocks + col_blocks),
        out_specs=(VMEM, VMEM, VMEM),
        compiler_params=PARAMS,
    )(scale, *audio, *text)
    row_others = [swap(row_sum, col_blocks * r) for r in range(1, row_blocks)]
    col_others = [swap(col_sum, c) for c in range(1, col_blocks)]
    parts = pl.pallas_call(
        functools.partial(grad_kernel, row_blocks, col_blocks),
        out_shape=[block_full if r == 0 else block_low for r in range(row_blocks)]
        + [block_full if c == 0 else block_low for c in range(col_blocks)],
        in_specs=[VMEM] * (1 + 2 * (row_blocks + col_blocks)),
        out_specs=[VMEM] * (row_blocks + col_blocks),
        compiler_params=PARAMS,
    )(grown, row_sum, col_sum, *row_others, *col_others, *audio, *text)
    audio_parts = [parts[0]] + [swap(parts[r], col_blocks * r) for r in range(1, row_blocks)]
    text_parts = [parts[row_blocks]] + [
        swap(parts[row_blocks + c], c) for c in range(1, col_blocks)
    ]
    return pl.pallas_call(
        functools.partial(final_kernel, row_blocks, col_blocks, pair_count),
        out_shape=(block_full, block_full),
        in_specs=[SMEM] + [VMEM] * (4 + row_blocks + col_blocks),
        out_specs=(VMEM, VMEM),
        compiler_params=PARAMS,
    )(scale, pooled, captions, audio_low, text_low, *audio_parts, *text_parts)


def solution(mesh):
    rows = P(("blk", "dp"))
    return jax.shard_map(
        local,
        mesh=mesh,
        in_specs=(rows, rows, rows, P(), P(), P(), rows, P()),
        out_specs=(rows, rows),
        check_vma=False,
    )
```

```python
import functools
import math

import jax
import jax.numpy as jnp
from jax import lax
from jax.experimental import pallas as pl
from jax.experimental.pallas import tpu as pltpu
from jax.sharding import PartitionSpec as P

epsilon = 1e-06
LOG2E = math.log2(math.e)
F32 = jnp.float32
BF16 = jnp.bfloat16
VMEM = pl.BlockSpec(memory_space=pltpu.VMEM)
SMEM = pl.BlockSpec(memory_space=pltpu.SMEM)
HBM = pl.BlockSpec(memory_space=pltpu.HBM)
PARAMS = pltpu.CompilerParams(vmem_limit_bytes=40 * 1024 * 1024)


def mm(left, right, left_dim=1, right_dim=0):
    return lax.dot_general(
        left, right, (((left_dim,), (right_dim,)), ((), ())), preferred_element_type=F32
    )


def in_hbm(array):
    return pltpu.with_memory_space_constraint(array, pltpu.HBM)


def swap(block, offset):
    count = lax.axis_size("blk")
    return lax.ppermute(block, "blk", [(i ^ offset, i) for i in range(count)])


def merge_kernel(count, offset, own_ref, other_ref, sum_ref):
    sum_ref[...] = own_ref[...]
    for k in range(count):
        sum_ref[pl.ds(k, 1), :] = own_ref[pl.ds(k, 1), :] + other_ref[pl.ds(k ^ offset, 1), :]


def total_sums(sums, count, stride):
    offset = 1
    while True:
        other = swap(sums, offset * stride)
        if 2 * offset >= count:
            return sums, other, offset
        sums = pl.pallas_call(
            functools.partial(merge_kernel, count, offset),
            out_shape=jax.ShapeDtypeStruct(sums.shape, F32),
            in_specs=[VMEM, VMEM],
            out_specs=VMEM,
            compiler_params=PARAMS,
        )(sums, other)
        offset *= 2


def blocks_of(refs, order, block):
    parts = [ref.at[pl.ds(at, block)] for ref in refs for at in range(0, ref.shape[0], block)]
    return [parts[order.index(k)] for k in range(len(parts))]


def unit_low(values):
    return values * lax.rsqrt(jnp.sum(values * values, axis=1, keepdims=True) + epsilon)


def text_kernel(captions_hbm, text_ref, captions_ref, sem):
    copy = pltpu.make_async_copy(captions_hbm, captions_ref, sem)
    copy.start()
    copy.wait()
    text_ref[...] = unit_low(captions_ref[...].astype(F32)).astype(BF16)


def frames_kernel(chunks, *refs):
    lengths_hbm, bias_hbm, first_hbm, second_hbm, frames_hbm, pooled_ref, audio_ref = refs[:7]
    lengths_ref, bias_ref, first_ref, second_ref, held, sems = refs[7:]
    copies = []
    at = 0
    for k, rows in enumerate(chunks):
        part = pl.ds(at, rows)
        copies.append(pltpu.make_async_copy(frames_hbm.at[part], held.at[part], sems.at[k]))
        at += rows
    extra = []
    for k, pair in enumerate(
        [
            (first_hbm, first_ref),
            (lengths_hbm, lengths_ref),
            (bias_hbm, bias_ref),
            (second_hbm, second_ref),
        ]
    ):
        extra.append(pltpu.make_async_copy(*pair, sems.at[len(chunks) + k]))
    first_copy, lengths_copy, bias_copy, second_copy = extra
    for copy in [lengths_copy, first_copy, copies[0], bias_copy, *copies[1:], second_copy]:
        copy.start()
    clips = lengths_ref.shape[1]
    lengths_copy.wait()
    lengths = lengths_ref[...].astype(F32)
    row_id = lax.broadcasted_iota(jnp.int32, (clips, clips), 0)
    col_id = lax.broadcasted_iota(jnp.int32, (clips, clips), 1)
    ends = jnp.sum(jnp.where(col_id <= row_id, lengths, 0.0), axis=1, keepdims=True)
    sizes = jnp.sum(jnp.where(col_id == row_id, lengths, 0.0), axis=1, keepdims=True)
    starts = ends - sizes
    live = jnp.sum(lengths_ref[...])
    bias_copy.wait()
    first_copy.wait()
    root = math.sqrt(2.0 / math.pi)

    def pooled_chunk(at, rows):
        before = mm(held[pl.ds(at, rows), :], first_ref[...]) + bias_ref[...]
        half = before * 0.5
        inner = before * (root + (root * 0.044715) * (before * before))
        active = (half + half * jnp.tanh(inner)).astype(BF16)
        place = lax.broadcasted_iota(jnp.int32, (clips, rows), 1).astype(F32) + float(at)
        onehot = jnp.where((place >= starts) & (place < ends), 1.0, 0.0).astype(BF16)
        return mm(onehot, active)

    at = 0
    for k, rows in enumerate(chunks):
        copies[k].wait()
        if k == 0:
            pooled_ref[...] = pooled_chunk(at, rows)
        else:

            @pl.when(live > at)
            def _():
                pooled_ref[...] += pooled_chunk(at, rows)

        at += rows
    second_copy.wait()
    total = pooled_ref[...]
    high = total.astype(BF16)
    rest = (total - high.astype(F32)).astype(BF16)
    second = second_ref[...]
    pooled = (mm(high, second) + mm(rest, second)) / sizes
    pooled_ref[...] = pooled
    audio_ref[...] = unit_low(pooled).astype(BF16)


def tile_kernel(row_blocks, order, scale_ref, *refs):
    audio = refs[:row_blocks]
    col_blocks = len(order)
    text = blocks_of(refs[row_blocks:-3], order, audio[0].shape[0])
    grown_ref, row_ref, col_ref = refs[-3:]
    block = audio[0].shape[0]
    factor = scale_ref[0, 0] * LOG2E
    row_ref[...] = jnp.zeros(row_ref.shape, F32)
    col_sums = [None] * col_blocks
    for r in range(row_blocks):
        rows = audio[r][...]
        partial = None
        for c in range(col_blocks):
            grown = jnp.exp2(mm(rows, text[c][...], 1, 1) * factor)
            grown_ref[pl.ds(r * block, block), pl.ds(c * block, block)] = grown
            down = jnp.sum(grown, axis=0, keepdims=True)
            col_sums[c] = down if r == 0 else col_sums[c] + down
            partial = grown if c == 0 else partial + grown
        row_ref[pl.ds(r, 1), :] = jnp.sum(partial.T, axis=0, keepdims=True)
    for c in range(col_blocks):
        col_ref[pl.ds(c, 1), :] = col_sums[c]


def grad_kernel(row_blocks, order, row_offset, col_offset, *refs):
    grown_ref, row_ref, row_other, col_ref, col_other = refs[:5]
    col_blocks = len(order)
    outs = refs[len(refs) - row_blocks - col_blocks :]
    audio_outs, text_outs = outs[:row_blocks], outs[row_blocks:]
    audio = refs[5 : 5 + row_blocks]
    block = audio[0].shape[0]
    text = blocks_of(refs[5 + row_blocks : len(refs) - len(outs)], order, block)

    def inverses(own, other, count, offset):
        return [
            1.0 / (own[pl.ds(k, 1), :] + other[pl.ds(k ^ offset, 1), :])
            for k in range(count)
        ]

    row_inverse = [
        jnp.broadcast_to(row, (block, block)).T for row in inverses(row_ref, row_other, row_blocks, row_offset)
    ]
    col_inverse = inverses(col_ref, col_other, col_blocks, col_offset)
    weights = [
        [
            (
                grown_ref[pl.ds(r * block, block), pl.ds(c * block, block)]
                * (row_inverse[r] + col_inverse[c])
            ).astype(BF16)
            for c in range(col_blocks)
        ]
        for r in range(row_blocks)
    ]
    for r in reversed(range(row_blocks)):
        total = sum(mm(weights[r][c], text[c][...]) for c in range(col_blocks))
        audio_outs[r][...] = total.astype(audio_outs[r].dtype)
    for c in reversed(range(col_blocks)):
        total = sum(mm(weights[r][c], audio[r][...], 0, 0) for r in range(row_blocks))
        text_outs[c][...] = total.astype(text_outs[c].dtype)


def final_kernel(pair_count, scale_ref, values_ref, partner_ref, *refs):
    parts, out_ref = refs[:-1], refs[-1]
    values = values_ref[...].astype(F32)
    total = parts[0][...] - 2.0 * partner_ref[...].astype(F32)
    for part in parts[1:]:
        total = total + part[...].astype(F32)
    total = total * (scale_ref[0, 0] / (2.0 * pair_count))
    inverse = lax.rsqrt(jnp.sum(values * values, axis=1, keepdims=True) + epsilon)
    unit = values * inverse
    along = jnp.sum(unit * total, axis=1, keepdims=True)
    out_ref[...] = (total - unit * along) * inverse


def local(frames, lengths, routes, w_first, b_first, w_second, captions, logit_scale):
    clips = lengths.shape[0]
    width = w_second.shape[1]
    group = lax.axis_size("blk")
    pair_count = clips * group * lax.axis_size("dp")
    col_blocks = min(4, group)
    row_blocks = group // col_blocks
    live_rows = min(routes.shape[1] * routes.shape[2], frames.shape[0])
    chunks = [live_rows // 2, live_rows // 4]
    chunks.append(live_rows - sum(chunks))
    scale = logit_scale.reshape(1, 1)
    block_low = jax.ShapeDtypeStruct((clips, width), BF16)
    block_full = jax.ShapeDtypeStruct((clips, width), F32)

    text_low = pl.pallas_call(
        text_kernel,
        out_shape=block_low,
        in_specs=[HBM],
        out_specs=VMEM,
        scratch_shapes=[pltpu.VMEM((clips, width), BF16), pltpu.SemaphoreType.DMA],
        compiler_params=PARAMS,
    )(in_hbm(captions))
    pooled, audio_low = pl.pallas_call(
        functools.partial(frames_kernel, chunks),
        out_shape=(block_full, block_low),
        in_specs=[HBM] * 5,
        out_specs=(VMEM, VMEM),
        scratch_shapes=[
            pltpu.VMEM((1, clips), lengths.dtype),
            pltpu.VMEM((1, width), F32),
            pltpu.VMEM(w_first.shape, BF16),
            pltpu.VMEM(w_second.shape, BF16),
            pltpu.VMEM((live_rows, frames.shape[1]), BF16),
            pltpu.SemaphoreType.DMA((len(chunks) + 4,)),
        ],
        compiler_params=PARAMS,
    )(
        *map(
            in_hbm,
            (lengths.reshape(1, clips), b_first.reshape(1, width), w_first, w_second, frames),
        )
    )
    text, order = [text_low], [0]
    offset = col_blocks // 2
    while offset:
        held = text_low
        if len(text) > 1:
            held, audio_low = lax.optimization_barrier((text, audio_low))
            held = jnp.concatenate(held, axis=0)
        text.append(swap(held, offset))
        order += [k ^ offset for k in order]
        offset //= 2
    audio = [audio_low] + [swap(audio_low, col_blocks * r) for r in range(1, row_blocks)]
    grown, row_sum, col_sum = pl.pallas_call(
        functools.partial(tile_kernel, row_blocks, order),
        out_shape=(
            jax.ShapeDtypeStruct((row_blocks * clips, col_blocks * clips), F32),
            jax.ShapeDtypeStruct((max(row_blocks, 8), clips), F32),
            jax.ShapeDtypeStruct((col_blocks, clips), F32),
        ),
        in_specs=[SMEM] + [VMEM] * (len(audio) + len(text)),
        out_specs=(VMEM, VMEM, VMEM),
        compiler_params=PARAMS,
    )(scale, *audio, *text)
    col_own, col_other, col_offset = total_sums(col_sum, col_blocks, 1)
    row_own, row_other, row_offset = total_sums(row_sum, row_blocks, col_blocks)
    parts = pl.pallas_call(
        functools.partial(grad_kernel, row_blocks, order, row_offset, col_offset),
        out_shape=[block_full if r == 0 else block_low for r in range(row_blocks)]
        + [block_full if c == 0 else block_low for c in range(col_blocks)],
        in_specs=[VMEM] * (5 + len(audio) + len(text)),
        out_specs=[VMEM] * (row_blocks + col_blocks),
        compiler_params=PARAMS,
    )(grown, row_own, row_other, col_own, col_other, *audio, *text)
    audio_parts = [parts[0]] + [swap(parts[r], col_blocks * r) for r in range(1, row_blocks)]
    text_parts = [parts[row_blocks]] + [
        swap(parts[row_blocks + c], c) for c in range(1, col_blocks)
    ]

    def final(values, partner, pieces):
        return pl.pallas_call(
            functools.partial(final_kernel, pair_count),
            out_shape=block_full,
            in_specs=[SMEM] + [VMEM] * (2 + len(pieces)),
            out_specs=VMEM,
            compiler_params=PARAMS,
        )(scale, values, partner, *pieces)

    return final(pooled, text_low, audio_parts), final(captions, audio_low, text_parts)


def solution(mesh):
    rows = P(("blk", "dp"))
    return jax.shard_map(
        local,
        mesh=mesh,
        in_specs=(rows, rows, rows, P(), P(), P(), rows, P()),
        out_specs=(rows, rows),
        check_vma=False,
    )
```

```python
import functools
import math

import jax
import jax.numpy as jnp
from jax import lax
from jax.experimental import pallas as pl
from jax.experimental.pallas import tpu as pltpu
from jax.sharding import PartitionSpec as P

epsilon = 1e-06
LOG2E = math.log2(math.e)
F32 = jnp.float32
BF16 = jnp.bfloat16
VMEM = pl.BlockSpec(memory_space=pltpu.VMEM)
SMEM = pl.BlockSpec(memory_space=pltpu.SMEM)
HBM = pl.BlockSpec(memory_space=pltpu.HBM)
PARAMS = pltpu.CompilerParams(vmem_limit_bytes=40 * 1024 * 1024)


def mm(left, right, left_dim=1, right_dim=0):
    return lax.dot_general(
        left, right, (((left_dim,), (right_dim,)), ((), ())), preferred_element_type=F32
    )


def in_hbm(array):
    return pltpu.with_memory_space_constraint(array, pltpu.HBM)


def swap(block, offset):
    count = lax.axis_size("blk")
    return lax.ppermute(block, "blk", [(i ^ offset, i) for i in range(count)])


def blocks_of(refs, offsets, block):
    parts = [ref.at[pl.ds(at, block)] for ref in refs for at in range(0, ref.shape[0], block)]
    return dict(zip(offsets, parts, strict=True))


def unit_low(values):
    return values * lax.rsqrt(jnp.sum(values * values, axis=1, keepdims=True) + epsilon)


def text_kernel(captions_hbm, text_ref, captions_ref, sem):
    copy = pltpu.make_async_copy(captions_hbm, captions_ref, sem)
    copy.start()
    copy.wait()
    text_ref[...] = unit_low(captions_ref[...].astype(F32)).astype(BF16)


def frames_kernel(chunks, *refs):
    lengths_hbm, bias_hbm, first_hbm, second_hbm, frames_hbm, pooled_ref, audio_ref = refs[:7]
    lengths_ref, bias_ref, first_ref, second_ref, held, sems = refs[7:]
    copies = []
    at = 0
    for k, rows in enumerate(chunks):
        part = pl.ds(at, rows)
        copies.append(pltpu.make_async_copy(frames_hbm.at[part], held.at[part], sems.at[k]))
        at += rows
    extra = []
    for k, pair in enumerate(
        [
            (first_hbm, first_ref),
            (lengths_hbm, lengths_ref),
            (bias_hbm, bias_ref),
            (second_hbm, second_ref),
        ]
    ):
        extra.append(pltpu.make_async_copy(*pair, sems.at[len(chunks) + k]))
    first_copy, lengths_copy, bias_copy, second_copy = extra
    for copy in [lengths_copy, first_copy, copies[0], bias_copy, *copies[1:], second_copy]:
        copy.start()
    clips = lengths_ref.shape[1]
    lengths_copy.wait()
    lengths = lengths_ref[...].astype(F32)
    row_id = lax.broadcasted_iota(jnp.int32, (clips, clips), 0)
    col_id = lax.broadcasted_iota(jnp.int32, (clips, clips), 1)
    ends = jnp.sum(jnp.where(col_id <= row_id, lengths, 0.0), axis=1, keepdims=True)
    sizes = jnp.sum(jnp.where(col_id == row_id, lengths, 0.0), axis=1, keepdims=True)
    starts = ends - sizes
    live = jnp.sum(lengths_ref[...])
    bias_copy.wait()
    first_copy.wait()
    root = math.sqrt(2.0 / math.pi)

    def pooled_chunk(at, rows):
        before = mm(held[pl.ds(at, rows), :], first_ref[...]) + bias_ref[...]
        half = before * 0.5
        inner = before * (root + (root * 0.044715) * (before * before))
        active = (half + half * jnp.tanh(inner)).astype(BF16)
        place = lax.broadcasted_iota(jnp.int32, (clips, rows), 1).astype(F32) + float(at)
        onehot = jnp.where((place >= starts) & (place < ends), 1.0, 0.0).astype(BF16)
        return mm(onehot, active)

    at = 0
    for k, rows in enumerate(chunks):
        copies[k].wait()
        if k == 0:
            pooled_ref[...] = pooled_chunk(at, rows)
        else:

            @pl.when(live > at)
            def _():
                pooled_ref[...] += pooled_chunk(at, rows)

        at += rows
    second_copy.wait()
    total = pooled_ref[...]
    high = total.astype(BF16)
    rest = (total - high.astype(F32)).astype(BF16)
    second = second_ref[...]
    pooled = (mm(high, second) + mm(rest, second)) / sizes
    pooled_ref[...] = pooled
    audio_ref[...] = unit_low(pooled).astype(BF16)


def tile_kernel(rows, columns, scale_ref, *refs):
    first_refs, last_refs = refs[: len(refs) - 3], refs[len(refs) - 3 :]
    grown_ref, row_ref, col_ref = last_refs
    block = row_ref.shape[1]
    held, at = [], 0
    for offsets in (rows, columns):
        taken, count = [], 0
        while count < len(offsets):
            taken.append(first_refs[at])
            count += first_refs[at].shape[0] // block
            at += 1
        held.append(blocks_of(taken, offsets, block))
    audio, text = held
    col_sums = [first_refs[at][pl.ds(c, 1), :] for c in range(len(columns))] if at < len(first_refs) else None
    factor = scale_ref[0, 0] * LOG2E
    for r, row in enumerate(rows):
        values = audio[row][...]
        partial = None
        downs = []
        for c, column in enumerate(columns):
            grown = jnp.exp2(mm(values, text[column][...], 1, 1) * factor)
            grown_ref[pl.ds(r * block, block), pl.ds(c * block, block)] = grown
            downs.append(jnp.sum(grown, axis=0, keepdims=True))
            partial = grown if c == 0 else partial + grown
        col_sums = downs if col_sums is None else [x + y for x, y in zip(col_sums, downs, strict=True)]
        row_ref[pl.ds(r, 1), :] = jnp.sum(partial.T, axis=0, keepdims=True)
    for c in range(len(columns)):
        col_ref[pl.ds(c, 1), :] = col_sums[c]


def grad_kernel(rows, columns, pick, *refs):
    block = refs[-1].shape[0]
    count = len(rows)
    grown, near = {}, 0
    held = 0
    while held < count:
        for k in range(refs[near].shape[0] // block):
            for c, column in enumerate(columns):
                grown[rows[held], column] = (near, k, c)
            held += 1
        near += 1
    row_ref, row_other, col_ref, col_other = refs[near : near + 4]
    audio_refs, text_refs, at = [], [], near + 4
    for store, wanted in ((audio_refs, len(rows)), (text_refs, len(columns))):
        total = 0
        while total < wanted:
            store.append(refs[at])
            total += refs[at].shape[0] // block
            at += 1
    audio, text = blocks_of(audio_refs, rows, block), blocks_of(text_refs, columns, block)
    audio_out, text_out = refs[at:]

    def inverse(offsets, offset, bit, own, other):
        here, there = (pl.ds(offsets.index(k), 1) for k in (offset, offset ^ bit))
        return 1.0 / (own[here, :] + other[there, :])

    def row_inverse(row):
        return jnp.broadcast_to(inverse(rows, row, 1, row_ref, row_other), (block, block)).T

    row_scale = {row: row_inverse(row) for row in rows}
    col_scale = {column: inverse(columns, column, 2, col_ref, col_other) for column in columns}

    def weights(row, column):
        index, k, c = grown[row, column]
        values = refs[index][pl.ds(k * block, block), pl.ds(c * block, block)]
        return (values * (row_scale[row] + col_scale[column])).astype(BF16)

    total = sum(mm(weights(pick[0], column), text[column][...]) for column in columns)
    audio_out[...] = total.astype(audio_out.dtype)
    total = sum(mm(weights(row, pick[1]), audio[row][...], 0, 0) for row in rows)
    text_out[...] = total.astype(text_out.dtype)


def final_kernel(pair_count, scale_ref, values_ref, partner_ref, *refs):
    parts, out_ref = refs[:-1], refs[-1]
    values = values_ref[...].astype(F32)
    total = parts[0][...] - 2.0 * partner_ref[...].astype(F32)
    for part in parts[1:]:
        total = total + part[...].astype(F32)
    total = total * (scale_ref[0, 0] / (2.0 * pair_count))
    inverse = lax.rsqrt(jnp.sum(values * values, axis=1, keepdims=True) + epsilon)
    unit = values * inverse
    along = jnp.sum(unit * total, axis=1, keepdims=True)
    out_ref[...] = (total - unit * along) * inverse


def local(frames, lengths, routes, w_first, b_first, w_second, captions, logit_scale):
    clips = lengths.shape[0]
    width = w_second.shape[1]
    group = lax.axis_size("blk")
    pair_count = clips * group * lax.axis_size("dp")
    shared_bits = [1 << k for k in range(2, group.bit_length() - 1)]
    live_rows = min(routes.shape[1] * routes.shape[2], frames.shape[0])
    chunks = [live_rows // 2, live_rows // 4]
    chunks.append(live_rows - sum(chunks))
    scale = logit_scale.reshape(1, 1)
    block_low = jax.ShapeDtypeStruct((clips, width), BF16)
    block_full = jax.ShapeDtypeStruct((clips, width), F32)

    text_low = pl.pallas_call(
        text_kernel,
        out_shape=block_low,
        in_specs=[HBM],
        out_specs=VMEM,
        scratch_shapes=[pltpu.VMEM((clips, width), BF16), pltpu.SemaphoreType.DMA],
        compiler_params=PARAMS,
    )(in_hbm(captions))
    pooled, audio_low = pl.pallas_call(
        functools.partial(frames_kernel, chunks),
        out_shape=(block_full, block_low),
        in_specs=[HBM] * 5,
        out_specs=(VMEM, VMEM),
        scratch_shapes=[
            pltpu.VMEM((1, clips), lengths.dtype),
            pltpu.VMEM((1, width), F32),
            pltpu.VMEM(w_first.shape, BF16),
            pltpu.VMEM(w_second.shape, BF16),
            pltpu.VMEM((live_rows, frames.shape[1]), BF16),
            pltpu.SemaphoreType.DMA((len(chunks) + 4,)),
        ],
        compiler_params=PARAMS,
    )(
        *map(
            in_hbm,
            (lengths.reshape(1, clips), b_first.reshape(1, width), w_first, w_second, frames),
        )
    )
    def joined(arrays):
        return arrays[0] if len(arrays) == 1 else jnp.concatenate(arrays, axis=0)

    def gathered(block):
        arrays, offsets = [block], [0]
        for bit in shared_bits:
            arrays.append(swap(joined(arrays), bit))
            offsets += [k ^ bit for k in offsets]
        return arrays, offsets

    text, columns = gathered(text_low)
    shared_text, _ = lax.optimization_barrier((text, audio_low))
    text += [swap(shared_text[0], 2), swap(joined(shared_text[1:]), 2)]
    columns += [k ^ 2 for k in columns]
    audio, rows = gathered(audio_low)
    audio.append(swap(audio_low, 1))
    early_rows = rows + [1]
    early_audio = list(audio)
    late_rows = [k ^ 1 for k in rows[1:]]
    late_audio = [swap(joined(audio[1:-1]), 1)]

    def tile(row_offsets, held, *sums):
        count = len(row_offsets)
        return pl.pallas_call(
            functools.partial(tile_kernel, row_offsets, columns),
            out_shape=(
                jax.ShapeDtypeStruct((count * clips, len(columns) * clips), F32),
                jax.ShapeDtypeStruct((count, clips), F32),
                jax.ShapeDtypeStruct((len(columns), clips), F32),
            ),
            in_specs=[SMEM] + [VMEM] * (len(held) + len(text) + len(sums)),
            out_specs=(VMEM, VMEM, VMEM),
            compiler_params=PARAMS,
        )(scale, *held, *text, *sums)

    early_grown, early_sum, col_sum = tile(early_rows, early_audio)
    late_grown, late_sum, col_sum = tile(late_rows, late_audio, col_sum)
    row_sum = jnp.concatenate([early_sum, late_sum], axis=0)
    row_other, col_other = swap(row_sum, 1), swap(col_sum, 2)
    rows, audio = early_rows + late_rows, early_audio + late_audio
    operands = [early_grown, late_grown, row_sum, row_other, col_sum, col_other, *audio, *text]

    def grads(pick, kind):
        return pl.pallas_call(
            functools.partial(grad_kernel, rows, columns, pick),
            out_shape=[kind, kind],
            in_specs=[VMEM] * len(operands),
            out_specs=[VMEM, VMEM],
            compiler_params=PARAMS,
        )(*operands)

    audio_sent, text_sent = grads((1, 2), block_low)
    text_parts, audio_parts = [swap(text_sent, 2)], [swap(audio_sent, 1)]
    audio_own, text_own = grads((0, 0), block_full)
    text_parts.insert(0, text_own)
    audio_parts.insert(0, audio_own)

    def final(values, partner, pieces):
        return pl.pallas_call(
            functools.partial(final_kernel, pair_count),
            out_shape=block_full,
            in_specs=[SMEM] + [VMEM] * (2 + len(pieces)),
            out_specs=VMEM,
            compiler_params=PARAMS,
        )(scale, values, partner, *pieces)

    return final(pooled, text_low, audio_parts), final(captions, audio_low, text_parts)


def solution(mesh):
    rows = P(("blk", "dp"))
    return jax.shard_map(
        local,
        mesh=mesh,
        in_specs=(rows, rows, rows, P(), P(), P(), rows, P()),
        out_specs=(rows, rows),
        check_vma=False,
    )
```

```python
import functools
import math

import jax
import jax.numpy as jnp
from jax import lax
from jax.experimental import pallas as pl
from jax.experimental.pallas import tpu as pltpu
from jax.sharding import PartitionSpec as P

epsilon = 1e-06
LOG2E = math.log2(math.e)
F32 = jnp.float32
BF16 = jnp.bfloat16
VMEM = pl.BlockSpec(memory_space=pltpu.VMEM)
SMEM = pl.BlockSpec(memory_space=pltpu.SMEM)
HBM = pl.BlockSpec(memory_space=pltpu.HBM)
PARAMS = pltpu.CompilerParams(vmem_limit_bytes=40 * 1024 * 1024)


def mm(left, right, left_dim=1, right_dim=0):
    return lax.dot_general(
        left, right, (((left_dim,), (right_dim,)), ((), ())), preferred_element_type=F32
    )


def in_hbm(array):
    return pltpu.with_memory_space_constraint(array, pltpu.HBM)


def swap(block, offset):
    count = lax.axis_size("blk")
    return lax.ppermute(block, "blk", [(i ^ offset, i) for i in range(count)])


def blocks_of(refs, offsets, block):
    parts = [ref.at[pl.ds(at, block)] for ref in refs for at in range(0, ref.shape[0], block)]
    return dict(zip(offsets, parts, strict=True))


def unit_low(values):
    return values * lax.rsqrt(jnp.sum(values * values, axis=1, keepdims=True) + epsilon)


def text_kernel(captions_hbm, text_ref, captions_ref, sem):
    copy = pltpu.make_async_copy(captions_hbm, captions_ref, sem)
    copy.start()
    copy.wait()
    text_ref[...] = unit_low(captions_ref[...].astype(F32)).astype(BF16)


def frames_kernel(chunks, *refs):
    lengths_hbm, bias_hbm, first_hbm, second_hbm, frames_hbm, pooled_ref, audio_ref = refs[:7]
    lengths_ref, bias_ref, first_ref, second_ref, held, sems = refs[7:]
    copies = []
    at = 0
    for k, rows in enumerate(chunks):
        part = pl.ds(at, rows)
        copies.append(pltpu.make_async_copy(frames_hbm.at[part], held.at[part], sems.at[k]))
        at += rows
    extra = []
    for k, pair in enumerate(
        [
            (first_hbm, first_ref),
            (lengths_hbm, lengths_ref),
            (bias_hbm, bias_ref),
            (second_hbm, second_ref),
        ]
    ):
        extra.append(pltpu.make_async_copy(*pair, sems.at[len(chunks) + k]))
    first_copy, lengths_copy, bias_copy, second_copy = extra
    for copy in [lengths_copy, first_copy, copies[0], bias_copy, *copies[1:], second_copy]:
        copy.start()
    clips = lengths_ref.shape[1]
    lengths_copy.wait()
    lengths = lengths_ref[...].astype(F32)
    row_id = lax.broadcasted_iota(jnp.int32, (clips, clips), 0)
    col_id = lax.broadcasted_iota(jnp.int32, (clips, clips), 1)
    ends = jnp.sum(jnp.where(col_id <= row_id, lengths, 0.0), axis=1, keepdims=True)
    sizes = jnp.sum(jnp.where(col_id == row_id, lengths, 0.0), axis=1, keepdims=True)
    starts = ends - sizes
    live = jnp.sum(lengths_ref[...])
    bias_copy.wait()
    first_copy.wait()
    root = math.sqrt(2.0 / math.pi)

    def pooled_chunk(at, rows):
        before = mm(held[pl.ds(at, rows), :], first_ref[...]) + bias_ref[...]
        half = before * 0.5
        inner = before * (root + (root * 0.044715) * (before * before))
        active = (half + half * jnp.tanh(inner)).astype(BF16)
        place = lax.broadcasted_iota(jnp.int32, (clips, rows), 1).astype(F32) + float(at)
        onehot = jnp.where((place >= starts) & (place < ends), 1.0, 0.0).astype(BF16)
        return mm(onehot, active)

    at = 0
    for k, rows in enumerate(chunks):
        copies[k].wait()
        if k == 0:
            pooled_ref[...] = pooled_chunk(at, rows)
        else:

            @pl.when(live > at)
            def _():
                pooled_ref[...] += pooled_chunk(at, rows)

        at += rows
    second_copy.wait()
    total = pooled_ref[...]
    high = total.astype(BF16)
    rest = (total - high.astype(F32)).astype(BF16)
    second = second_ref[...]
    pooled = (mm(high, second) + mm(rest, second)) / sizes
    pooled_ref[...] = pooled
    audio_ref[...] = unit_low(pooled).astype(BF16)


def tile_kernel(rows, columns, scale_ref, *refs):
    first_refs, last_refs = refs[: len(refs) - 3], refs[len(refs) - 3 :]
    grown_ref, row_ref, col_ref = last_refs
    block = row_ref.shape[1]
    held, at = [], 0
    for offsets in (rows, columns):
        taken, count = [], 0
        while count < len(offsets):
            taken.append(first_refs[at])
            count += first_refs[at].shape[0] // block
            at += 1
        held.append(blocks_of(taken, offsets, block))
    audio, text = held
    col_sums = [first_refs[at][pl.ds(c, 1), :] for c in range(len(columns))] if at < len(first_refs) else None
    factor = scale_ref[0, 0] * LOG2E
    for r, row in enumerate(rows):
        values = audio[row][...]
        partial = None
        downs = []
        for c, column in enumerate(columns):
            grown = jnp.exp2(mm(values, text[column][...], 1, 1) * factor)
            grown_ref[pl.ds(r * block, block), pl.ds(c * block, block)] = grown
            downs.append(jnp.sum(grown, axis=0, keepdims=True))
            partial = grown if c == 0 else partial + grown
        col_sums = downs if col_sums is None else [x + y for x, y in zip(col_sums, downs, strict=True)]
        row_ref[pl.ds(r, 1), :] = jnp.sum(partial.T, axis=0, keepdims=True)
    for c in range(len(columns)):
        col_ref[pl.ds(c, 1), :] = col_sums[c]


def grad_kernel(rows, columns, pick, *refs):
    block = refs[-1].shape[0]
    count = len(rows)
    grown, near = {}, 0
    held = 0
    while held < count:
        for k in range(refs[near].shape[0] // block):
            for c, column in enumerate(columns):
                grown[rows[held], column] = (near, k, c)
            held += 1
        near += 1
    row_ref, row_other, col_ref, col_other = refs[near : near + 4]
    audio_refs, text_refs, at = [], [], near + 4
    for store, wanted in ((audio_refs, len(rows)), (text_refs, len(columns))):
        total = 0
        while total < wanted:
            store.append(refs[at])
            total += refs[at].shape[0] // block
            at += 1
    audio, text = blocks_of(audio_refs, rows, block), blocks_of(text_refs, columns, block)
    audio_out, text_out = refs[at:]

    def inverse(offsets, offset, bit, own, other):
        here, there = (pl.ds(offsets.index(k), 1) for k in (offset, offset ^ bit))
        return 1.0 / (own[here, :] + other[there, :])

    def row_inverse(row):
        return jnp.broadcast_to(inverse(rows, row, 1, row_ref, row_other), (block, block)).T

    row_scale = {row: row_inverse(row) for row in rows}
    col_scale = {column: inverse(columns, column, 2, col_ref, col_other) for column in columns}

    def weights(row, column):
        index, k, c = grown[row, column]
        values = refs[index][pl.ds(k * block, block), pl.ds(c * block, block)]
        return (values * (row_scale[row] + col_scale[column])).astype(BF16)

    total = sum(mm(weights(pick[0], column), text[column][...]) for column in columns)
    audio_out[...] = total.astype(audio_out.dtype)
    total = sum(mm(weights(row, pick[1]), audio[row][...], 0, 0) for row in rows)
    text_out[...] = total.astype(text_out.dtype)


def final_kernel(pair_count, count, scale_ref, *refs):
    factor = scale_ref[0, 0] / (2.0 * pair_count)
    copies = []
    outs, stages, sems = refs[2 * count :][:2], refs[2 * count + 2 :][:2], refs[-1]
    for side in range(2):
        values_ref, partner_ref, *parts = refs[side * count : (side + 1) * count]
        values = values_ref[...].astype(F32)
        total = parts[0][...] - 2.0 * partner_ref[...].astype(F32)
        for part in parts[1:]:
            total = total + part[...].astype(F32)
        total = total * factor
        inverse = lax.rsqrt(jnp.sum(values * values, axis=1, keepdims=True) + epsilon)
        unit = values * inverse
        along = jnp.sum(unit * total, axis=1, keepdims=True)
        stages[side][...] = (total - unit * along) * inverse
        copies.append(pltpu.make_async_copy(stages[side], outs[side], sems.at[side]))
        copies[-1].start()
    for copy in copies:
        copy.wait()


def local(frames, lengths, routes, w_first, b_first, w_second, captions, logit_scale):
    clips = lengths.shape[0]
    width = w_second.shape[1]
    group = lax.axis_size("blk")
    pair_count = clips * group * lax.axis_size("dp")
    shared_bits = [1 << k for k in range(2, group.bit_length() - 1)]
    live_rows = min(routes.shape[1] * routes.shape[2], frames.shape[0])
    chunks = [live_rows // 2, live_rows // 4]
    chunks.append(live_rows - sum(chunks))
    scale = logit_scale.reshape(1, 1)
    block_low = jax.ShapeDtypeStruct((clips, width), BF16)
    block_full = jax.ShapeDtypeStruct((clips, width), F32)

    text_low = pl.pallas_call(
        text_kernel,
        out_shape=block_low,
        in_specs=[HBM],
        out_specs=VMEM,
        scratch_shapes=[pltpu.VMEM((clips, width), BF16), pltpu.SemaphoreType.DMA],
        compiler_params=PARAMS,
    )(in_hbm(captions))
    pooled, audio_low = pl.pallas_call(
        functools.partial(frames_kernel, chunks),
        out_shape=(block_full, block_low),
        in_specs=[HBM] * 5,
        out_specs=(VMEM, VMEM),
        scratch_shapes=[
            pltpu.VMEM((1, clips), lengths.dtype),
            pltpu.VMEM((1, width), F32),
            pltpu.VMEM(w_first.shape, BF16),
            pltpu.VMEM(w_second.shape, BF16),
            pltpu.VMEM((live_rows, frames.shape[1]), BF16),
            pltpu.SemaphoreType.DMA((len(chunks) + 4,)),
        ],
        compiler_params=PARAMS,
    )(
        *map(
            in_hbm,
            (lengths.reshape(1, clips), b_first.reshape(1, width), w_first, w_second, frames),
        )
    )
    def joined(arrays):
        return arrays[0] if len(arrays) == 1 else jnp.concatenate(arrays, axis=0)

    def gathered(block):
        arrays, offsets = [block], [0]
        for bit in shared_bits:
            arrays.append(swap(joined(arrays), bit))
            offsets += [k ^ bit for k in offsets]
        return arrays, offsets

    text, columns = gathered(text_low)
    shared_text, _ = lax.optimization_barrier((text, audio_low))
    text += [swap(text_low, 2), swap(joined(shared_text[1:]), 2)]
    columns += [k ^ 2 for k in columns]
    audio, rows = gathered(audio_low)
    audio.append(swap(audio_low, 1))
    early_rows = rows + [1]
    early_audio = list(audio)
    late_rows = [k ^ 1 for k in rows[1:]]
    late_audio = [swap(joined(audio[1:-1]), 1)]

    def tile(row_offsets, held, *sums):
        count = len(row_offsets)
        return pl.pallas_call(
            functools.partial(tile_kernel, row_offsets, columns),
            out_shape=(
                jax.ShapeDtypeStruct((count * clips, len(columns) * clips), F32),
                jax.ShapeDtypeStruct((count, clips), F32),
                jax.ShapeDtypeStruct((len(columns), clips), F32),
            ),
            in_specs=[SMEM] + [VMEM] * (len(held) + len(text) + len(sums)),
            out_specs=(VMEM, VMEM, VMEM),
            compiler_params=PARAMS,
        )(scale, *held, *text, *sums)

    early_grown, early_sum, col_sum = tile(early_rows, early_audio)
    late_grown, late_sum, col_sum = tile(late_rows, late_audio, col_sum)
    row_sum = jnp.concatenate([early_sum, late_sum], axis=0)
    row_other, col_other = swap(row_sum, 1), swap(col_sum, 2)
    rows, audio = early_rows + late_rows, early_audio + late_audio
    operands = [early_grown, late_grown, row_sum, row_other, col_sum, col_other, *audio, *text]

    def grads(pick, kind):
        return pl.pallas_call(
            functools.partial(grad_kernel, rows, columns, pick),
            out_shape=[kind, kind],
            in_specs=[VMEM] * len(operands),
            out_specs=[VMEM, VMEM],
            compiler_params=PARAMS,
        )(*operands)

    audio_sent, text_sent = grads((1, 2), block_low)
    text_parts, audio_parts = [swap(text_sent, 2)], [swap(audio_sent, 1)]
    audio_own, text_own = grads((0, 0), block_full)
    text_parts.insert(0, text_own)
    audio_parts.insert(0, audio_own)

    sides = [pooled, text_low, *audio_parts, captions, audio_low, *text_parts]
    return pl.pallas_call(
        functools.partial(final_kernel, pair_count, len(sides) // 2),
        out_shape=(block_full, block_full),
        in_specs=[SMEM] + [VMEM] * len(sides),
        out_specs=(HBM, HBM),
        scratch_shapes=[
            pltpu.VMEM((clips, width), F32),
            pltpu.VMEM((clips, width), F32),
            pltpu.SemaphoreType.DMA((2,)),
        ],
        compiler_params=PARAMS,
    )(scale, *sides)


def solution(mesh):
    rows = P(("blk", "dp"))
    return jax.shard_map(
        local,
        mesh=mesh,
        in_specs=(rows, rows, rows, P(), P(), P(), rows, P()),
        out_specs=(rows, rows),
        check_vma=False,
    )
```

```python
import functools
import math

import jax
import jax.numpy as jnp
from jax import lax
from jax.experimental import pallas as pl
from jax.experimental.pallas import tpu as pltpu
from jax.sharding import PartitionSpec as P

epsilon = 1e-06
LOG2E = math.log2(math.e)
F32 = jnp.float32
BF16 = jnp.bfloat16
VMEM = pl.BlockSpec(memory_space=pltpu.VMEM)
SMEM = pl.BlockSpec(memory_space=pltpu.SMEM)
HBM = pl.BlockSpec(memory_space=pltpu.HBM)
PARAMS = pltpu.CompilerParams(vmem_limit_bytes=40 * 1024 * 1024)


def mm(left, right, left_dim=1, right_dim=0):
    return lax.dot_general(
        left, right, (((left_dim,), (right_dim,)), ((), ())), preferred_element_type=F32
    )


def in_hbm(array):
    return pltpu.with_memory_space_constraint(array, pltpu.HBM)


def swap(block, offset):
    count = lax.axis_size("blk")
    return lax.ppermute(block, "blk", [(i ^ offset, i) for i in range(count)])


def blocks_of(refs, offsets, block):
    parts = [ref.at[pl.ds(at, block)] for ref in refs for at in range(0, ref.shape[0], block)]
    return dict(zip(offsets, parts, strict=True))


def unit_low(values):
    return values * lax.rsqrt(jnp.sum(values * values, axis=1, keepdims=True) + epsilon)


def frames_kernel(chunks, *refs):
    lengths_hbm, bias_hbm, first_hbm, second_hbm, frames_hbm, pooled_ref, audio_ref = refs[:7]
    lengths_ref, bias_ref, first_ref, second_ref, held, sems = refs[7:]
    copies = []
    at = 0
    for k, rows in enumerate(chunks):
        part = pl.ds(at, rows)
        copies.append(pltpu.make_async_copy(frames_hbm.at[part], held.at[part], sems.at[k]))
        at += rows
    extra = []
    for k, pair in enumerate(
        [
            (first_hbm, first_ref),
            (lengths_hbm, lengths_ref),
            (bias_hbm, bias_ref),
            (second_hbm, second_ref),
        ]
    ):
        extra.append(pltpu.make_async_copy(*pair, sems.at[len(chunks) + k]))
    first_copy, lengths_copy, bias_copy, second_copy = extra
    for copy in [lengths_copy, first_copy, copies[0], bias_copy, *copies[1:], second_copy]:
        copy.start()
    clips = lengths_ref.shape[1]
    lengths_copy.wait()
    lengths = lengths_ref[...].astype(F32)
    row_id = lax.broadcasted_iota(jnp.int32, (clips, clips), 0)
    col_id = lax.broadcasted_iota(jnp.int32, (clips, clips), 1)
    ends = jnp.sum(jnp.where(col_id <= row_id, lengths, 0.0), axis=1, keepdims=True)
    sizes = jnp.sum(jnp.where(col_id == row_id, lengths, 0.0), axis=1, keepdims=True)
    starts = ends - sizes
    live = jnp.sum(lengths_ref[...])
    bias_copy.wait()
    first_copy.wait()
    root = math.sqrt(2.0 / math.pi)

    def pooled_chunk(at, rows):
        before = mm(held[pl.ds(at, rows), :], first_ref[...]) + bias_ref[...]
        half = before * 0.5
        inner = before * (root + (root * 0.044715) * (before * before))
        active = (half + half * jnp.tanh(inner)).astype(BF16)
        place = lax.broadcasted_iota(jnp.int32, (clips, rows), 1).astype(F32) + float(at)
        onehot = jnp.where((place >= starts) & (place < ends), 1.0, 0.0).astype(BF16)
        return mm(onehot, active)

    at = 0
    for k, rows in enumerate(chunks):
        copies[k].wait()
        if k == 0:
            pooled_ref[...] = pooled_chunk(at, rows)
        else:

            @pl.when(live > at)
            def _():
                pooled_ref[...] += pooled_chunk(at, rows)

        at += rows
    second_copy.wait()
    total = pooled_ref[...]
    high = total.astype(BF16)
    rest = (total - high.astype(F32)).astype(BF16)
    second = second_ref[...]
    pooled = (mm(high, second) + mm(rest, second)) / sizes
    pooled_ref[...] = pooled
    audio_ref[...] = unit_low(pooled).astype(BF16)


def tile_kernel(rows, columns, audio_refs, text, col_sums, scale, grown_ref, row_ref, col_ref):
    block = row_ref.shape[1]
    audio = blocks_of(audio_refs, rows, block)
    for r, row in enumerate(rows):
        values = audio[row][...]
        partial = None
        downs = []
        for c in range(len(columns)):
            grown = jnp.exp2(mm(values, text[c], 1, 1) * (scale * LOG2E))
            grown_ref[pl.ds(r * block, block), pl.ds(c * block, block)] = grown
            downs.append(jnp.sum(grown, axis=0, keepdims=True))
            partial = grown if c == 0 else partial + grown
        col_sums = downs if col_sums is None else [x + y for x, y in zip(col_sums, downs, strict=True)]
        row_ref[pl.ds(r, 1), :] = jnp.sum(partial.T, axis=0, keepdims=True)
    for c in range(len(columns)):
        col_ref[pl.ds(c, 1), :] = col_sums[c]


def early_tile_kernel(rows, columns, audio_count, scale_ref, *refs):
    grown_ref, row_ref, col_ref, low_ref = refs[len(refs) - 4 :]
    block = row_ref.shape[1]
    raw = blocks_of(refs[audio_count : len(refs) - 4], columns, block)
    text = []
    for c, column in enumerate(columns):
        text.append(unit_low(raw[column][...].astype(F32)).astype(BF16))
        low_ref[pl.ds(c * block, block), :] = text[c]
    audio = refs[:audio_count]
    tile_kernel(rows, columns, audio, text, None, scale_ref[0, 0], grown_ref, row_ref, col_ref)


def late_tile_kernel(rows, columns, scale_ref, *refs):
    low_ref, sums_ref, grown_ref, row_ref, col_ref = refs[len(refs) - 5 :]
    block = row_ref.shape[1]
    text = [low_ref[pl.ds(c * block, block), :] for c in range(len(columns))]
    sums = [sums_ref[pl.ds(c, 1), :] for c in range(len(columns))]
    audio = refs[: len(refs) - 5]
    tile_kernel(rows, columns, audio, text, sums, scale_ref[0, 0], grown_ref, row_ref, col_ref)


def grad_kernel(rows, columns, row_bit, col_bit, pick, *refs):
    block = refs[len(refs) - 1].shape[0]
    count = len(rows)
    grown, near = {}, 0
    held = 0
    while held < count:
        for k in range(refs[near].shape[0] // block):
            for c, column in enumerate(columns):
                grown[rows[held], column] = (near, k, c)
            held += 1
        near += 1
    row_ref, row_other, col_ref, col_other = refs[near : near + 4]
    audio_refs, text_refs, at = [], [], near + 4
    for store, wanted in ((audio_refs, len(rows)), (text_refs, len(columns))):
        total = 0
        while total < wanted:
            store.append(refs[at])
            total += refs[at].shape[0] // block
            at += 1
    audio, text = blocks_of(audio_refs, rows, block), blocks_of(text_refs, columns, block)
    audio_out, text_out = refs[at:]

    def inverse(offsets, offset, bit, own, other):
        here, there = (pl.ds(offsets.index(k), 1) for k in (offset, offset ^ bit))
        return 1.0 / (own[here, :] + other[there, :])

    def row_inverse(row):
        return jnp.broadcast_to(inverse(rows, row, row_bit, row_ref, row_other), (block, block)).T

    row_scale = {row: row_inverse(row) for row in rows}
    col_scale = {column: inverse(columns, column, col_bit, col_ref, col_other) for column in columns}

    def weights(row, column):
        index, k, c = grown[row, column]
        values = refs[index][pl.ds(k * block, block), pl.ds(c * block, block)]
        return (values * (row_scale[row] + col_scale[column])).astype(BF16)

    total = sum(mm(weights(pick[0], column), text[column][...]) for column in columns)
    audio_out[...] = total.astype(audio_out.dtype)
    total = sum(mm(weights(row, pick[1]), audio[row][...], 0, 0) for row in rows)
    text_out[...] = total.astype(text_out.dtype)


def final_kernel(pair_count, count, scale_ref, *refs):
    factor = scale_ref[0, 0] / (2.0 * pair_count)
    copies = []
    outs, stages, sems = refs[2 * count :][:2], refs[2 * count + 2 :][:2], refs[-1]
    for side in range(2):
        values_ref, partner_ref, *parts = refs[side * count : (side + 1) * count]
        values = values_ref[...].astype(F32)
        total = parts[0][...] - 2.0 * partner_ref[pl.ds(0, values.shape[0]), :].astype(F32)
        for part in parts[1:]:
            total = total + part[...].astype(F32)
        total = total * factor
        inverse = lax.rsqrt(jnp.sum(values * values, axis=1, keepdims=True) + epsilon)
        unit = values * inverse
        along = jnp.sum(unit * total, axis=1, keepdims=True)
        stages[side][...] = (total - unit * along) * inverse
        copies.append(pltpu.make_async_copy(stages[side], outs[side], sems.at[side]))
        copies[-1].start()
    for copy in copies:
        copy.wait()


def local(frames, lengths, routes, w_first, b_first, w_second, captions, logit_scale):
    clips = lengths.shape[0]
    width = w_second.shape[1]
    group = lax.axis_size("blk")
    pair_count = clips * group * lax.axis_size("dp")
    bits = [1 << k for k in range(group.bit_length() - 1)]
    row_bit, col_bit = bits[1], bits[0]
    shared_bits = [bit for bit in bits if bit not in (row_bit, col_bit)]
    live_rows = min(routes.shape[1] * routes.shape[2], frames.shape[0])
    chunks = [live_rows // 2, live_rows // 4]
    chunks.append(live_rows - sum(chunks))
    scale = logit_scale.reshape(1, 1)
    block_low = jax.ShapeDtypeStruct((clips, width), BF16)
    block_full = jax.ShapeDtypeStruct((clips, width), F32)

    pooled, audio_low = pl.pallas_call(
        functools.partial(frames_kernel, chunks),
        out_shape=(block_full, block_low),
        in_specs=[HBM] * 5,
        out_specs=(VMEM, VMEM),
        scratch_shapes=[
            pltpu.VMEM((1, clips), lengths.dtype),
            pltpu.VMEM((1, width), F32),
            pltpu.VMEM(w_first.shape, BF16),
            pltpu.VMEM(w_second.shape, BF16),
            pltpu.VMEM((live_rows, frames.shape[1]), BF16),
            pltpu.SemaphoreType.DMA((len(chunks) + 4,)),
        ],
        compiler_params=PARAMS,
    )(
        *map(
            in_hbm,
            (lengths.reshape(1, clips), b_first.reshape(1, width), w_first, w_second, frames),
        )
    )
    def joined(arrays):
        return arrays[0] if len(arrays) == 1 else jnp.concatenate(arrays, axis=0)

    def gathered(block):
        arrays, offsets = [block], [0]
        for bit in shared_bits:
            arrays.append(swap(joined(arrays), bit))
            offsets += [k ^ bit for k in offsets]
        return arrays, offsets

    text, columns = gathered(captions)
    shared_text, _ = lax.optimization_barrier((text, audio_low))
    text += [swap(captions, col_bit), swap(joined(shared_text[1:]), col_bit)]
    columns += [k ^ col_bit for k in columns]
    audio, rows = gathered(audio_low)
    audio.append(swap(audio_low, row_bit))
    early_rows = rows + [row_bit]
    early_audio = list(audio)
    late_rows = [k ^ row_bit for k in rows[1:]]
    late_audio = [swap(joined(audio[1:-1]), row_bit)]

    def tile_shapes(row_offsets):
        count = len(row_offsets)
        return (
            jax.ShapeDtypeStruct((count * clips, len(columns) * clips), F32),
            jax.ShapeDtypeStruct((count, clips), F32),
            jax.ShapeDtypeStruct((len(columns), clips), F32),
        )

    early_grown, early_sum, col_sum, text_low = pl.pallas_call(
        functools.partial(early_tile_kernel, early_rows, columns, len(early_audio)),
        out_shape=(
            *tile_shapes(early_rows),
            jax.ShapeDtypeStruct((len(columns) * clips, width), BF16),
        ),
        in_specs=[SMEM] + [VMEM] * (len(early_audio) + len(text)),
        out_specs=[VMEM] * 4,
        compiler_params=PARAMS,
    )(scale, *early_audio, *text)
    late_grown, late_sum, col_sum = pl.pallas_call(
        functools.partial(late_tile_kernel, late_rows, columns),
        out_shape=tile_shapes(late_rows),
        in_specs=[SMEM] + [VMEM] * (len(late_audio) + 2),
        out_specs=[VMEM] * 3,
        compiler_params=PARAMS,
    )(scale, *late_audio, text_low, col_sum)
    row_sum = jnp.concatenate([early_sum, late_sum], axis=0)
    row_other, col_other = swap(row_sum, row_bit), swap(col_sum, col_bit)
    rows, audio = early_rows + late_rows, early_audio + late_audio
    operands = [early_grown, late_grown, row_sum, row_other, col_sum, col_other, *audio, text_low]

    def grads(pick, kind):
        return pl.pallas_call(
            functools.partial(grad_kernel, rows, columns, row_bit, col_bit, pick),
            out_shape=[kind, kind],
            in_specs=[VMEM] * len(operands),
            out_specs=[VMEM, VMEM],
            compiler_params=PARAMS,
        )(*operands)

    audio_sent, text_sent = grads((row_bit, col_bit), block_low)
    text_parts, audio_parts = [swap(text_sent, col_bit)], [swap(audio_sent, row_bit)]
    audio_own, text_own = grads((0, 0), block_full)
    text_parts.insert(0, text_own)
    audio_parts.insert(0, audio_own)

    sides = [pooled, text_low, *audio_parts, captions, audio_low, *text_parts]
    return pl.pallas_call(
        functools.partial(final_kernel, pair_count, len(sides) // 2),
        out_shape=(block_full, block_full),
        in_specs=[SMEM] + [VMEM] * len(sides),
        out_specs=(HBM, HBM),
        scratch_shapes=[
            pltpu.VMEM((clips, width), F32),
            pltpu.VMEM((clips, width), F32),
            pltpu.SemaphoreType.DMA((2,)),
        ],
        compiler_params=PARAMS,
    )(scale, *sides)


def solution(mesh):
    rows = P(("blk", "dp"))
    return jax.shard_map(
        local,
        mesh=mesh,
        in_specs=(rows, rows, rows, P(), P(), P(), rows, P()),
        out_specs=(rows, rows),
        check_vma=False,
    )
```

```python
import functools
import math

import jax
import jax.numpy as jnp
from jax import lax
from jax.experimental import pallas as pl
from jax.experimental.pallas import tpu as pltpu
from jax.sharding import PartitionSpec as P

epsilon = 1e-06
LOG2E = math.log2(math.e)
F32 = jnp.float32
BF16 = jnp.bfloat16
VMEM = pl.BlockSpec(memory_space=pltpu.VMEM)
SMEM = pl.BlockSpec(memory_space=pltpu.SMEM)
HBM = pl.BlockSpec(memory_space=pltpu.HBM)
PARAMS = pltpu.CompilerParams(vmem_limit_bytes=40 * 1024 * 1024)


def mm(left, right, left_dim=1, right_dim=0):
    return lax.dot_general(
        left, right, (((left_dim,), (right_dim,)), ((), ())), preferred_element_type=F32
    )


def in_hbm(array):
    return pltpu.with_memory_space_constraint(array, pltpu.HBM)


def swap(block, offset):
    count = lax.axis_size("blk")
    return lax.ppermute(block, "blk", [(i ^ offset, i) for i in range(count)])


def blocks_of(refs, offsets, block):
    parts = [ref.at[pl.ds(at, block)] for ref in refs for at in range(0, ref.shape[0], block)]
    return dict(zip(offsets, parts, strict=True))


def unit_low(values):
    return values * lax.rsqrt(jnp.sum(values * values, axis=1, keepdims=True) + epsilon)


def frames_kernel(chunks, *refs):
    lengths_hbm, bias_hbm, first_hbm, second_hbm, frames_hbm, pooled_ref, audio_ref = refs[:7]
    lengths_ref, bias_ref, first_ref, second_ref, held, sems = refs[7:]
    copies = []
    at = 0
    for k, rows in enumerate(chunks):
        part = pl.ds(at, rows)
        copies.append(pltpu.make_async_copy(frames_hbm.at[part], held.at[part], sems.at[k]))
        at += rows
    extra = []
    for k, pair in enumerate(
        [
            (first_hbm, first_ref),
            (lengths_hbm, lengths_ref),
            (bias_hbm, bias_ref),
            (second_hbm, second_ref),
        ]
    ):
        extra.append(pltpu.make_async_copy(*pair, sems.at[len(chunks) + k]))
    first_copy, lengths_copy, bias_copy, second_copy = extra
    for copy in [lengths_copy, first_copy, copies[0], bias_copy, *copies[1:], second_copy]:
        copy.start()
    clips = lengths_ref.shape[1]
    lengths_copy.wait()
    lengths = lengths_ref[...].astype(F32)
    row_id = lax.broadcasted_iota(jnp.int32, (clips, clips), 0)
    col_id = lax.broadcasted_iota(jnp.int32, (clips, clips), 1)
    ends = jnp.sum(jnp.where(col_id <= row_id, lengths, 0.0), axis=1, keepdims=True)
    sizes = jnp.sum(jnp.where(col_id == row_id, lengths, 0.0), axis=1, keepdims=True)
    starts = ends - sizes
    live = jnp.sum(lengths_ref[...])
    bias_copy.wait()
    first_copy.wait()
    root = math.sqrt(2.0 / math.pi)

    def pooled_chunk(at, rows):
        before = mm(held[pl.ds(at, rows), :], first_ref[...]) + bias_ref[...]
        half = before * 0.5
        inner = before * (root + (root * 0.044715) * (before * before))
        active = (half + half * jnp.tanh(inner)).astype(BF16)
        place = lax.broadcasted_iota(jnp.int32, (clips, rows), 1).astype(F32) + float(at)
        onehot = jnp.where((place >= starts) & (place < ends), 1.0, 0.0).astype(BF16)
        return mm(onehot, active)

    at = 0
    for k, rows in enumerate(chunks):
        copies[k].wait()
        if k == 0:
            pooled_ref[...] = pooled_chunk(at, rows)
        else:

            @pl.when(live > at)
            def _():
                pooled_ref[...] += pooled_chunk(at, rows)

        at += rows
    second_copy.wait()
    total = pooled_ref[...]
    high = total.astype(BF16)
    rest = (total - high.astype(F32)).astype(BF16)
    second = second_ref[...]
    pooled = (mm(high, second) + mm(rest, second)) / sizes
    pooled_ref[...] = pooled
    audio_ref[...] = unit_low(pooled).astype(BF16)


def tile_kernel(rows, columns, audio_refs, text, col_sums, scale, grown_ref, row_ref, col_ref):
    block = row_ref.shape[1]
    audio = blocks_of(audio_refs, rows, block)
    for r, row in enumerate(rows):
        values = audio[row][...]
        partial = None
        downs = []
        for c in range(len(columns)):
            grown = jnp.exp2(mm(values, text[c], 1, 1) * (scale * LOG2E))
            grown_ref[pl.ds(r * block, block), pl.ds(c * block, block)] = grown
            downs.append(jnp.sum(grown, axis=0, keepdims=True))
            partial = grown if c == 0 else partial + grown
        col_sums = downs if col_sums is None else [x + y for x, y in zip(col_sums, downs, strict=True)]
        row_ref[pl.ds(r, 1), :] = jnp.sum(partial.T, axis=0, keepdims=True)
    for c in range(len(columns)):
        col_ref[pl.ds(c, 1), :] = col_sums[c]


def early_tile_kernel(rows, columns, audio_count, scale_ref, *refs):
    grown_ref, row_ref, col_ref, low_ref = refs[len(refs) - 4 :]
    block = row_ref.shape[1]
    raw = blocks_of(refs[audio_count : len(refs) - 4], columns, block)
    text = []
    for c, column in enumerate(columns):
        text.append(unit_low(raw[column][...].astype(F32)).astype(BF16))
        low_ref[pl.ds(c * block, block), :] = text[c]
    audio = refs[:audio_count]
    tile_kernel(rows, columns, audio, text, None, scale_ref[0, 0], grown_ref, row_ref, col_ref)


def late_tile_kernel(rows, columns, scale_ref, *refs):
    low_ref, sums_ref, grown_ref, row_ref, col_ref = refs[len(refs) - 5 :]
    block = row_ref.shape[1]
    text = [low_ref[pl.ds(c * block, block), :] for c in range(len(columns))]
    sums = [sums_ref[pl.ds(c, 1), :] for c in range(len(columns))]
    audio = refs[: len(refs) - 5]
    tile_kernel(rows, columns, audio, text, sums, scale_ref[0, 0], grown_ref, row_ref, col_ref)


def grad_kernel(rows, columns, row_bit, col_bit, pick, pair_count, scale_ref, *refs):
    block = refs[1].shape[1] // len(columns)
    count = len(rows)
    grown, near = {}, 0
    held = 0
    while held < count:
        for k in range(refs[near].shape[0] // block):
            for c, column in enumerate(columns):
                grown[rows[held], column] = (near, k, c)
            held += 1
        near += 1
    row_ref, row_other, col_ref, col_other = refs[near : near + 4]
    audio_refs, text_refs, at = [], [], near + 4
    for store, wanted in ((audio_refs, len(rows)), (text_refs, len(columns))):
        total = 0
        while total < wanted:
            store.append(refs[at])
            total += refs[at].shape[0] // block
            at += 1
    audio, text = blocks_of(audio_refs, rows, block), blocks_of(text_refs, columns, block)
    sources, outs = ([], refs[at:]) if pair_count is None else (refs[at : at + 2], refs[at + 2 :])

    def inverse(offsets, offset, bit, own, other):
        here, there = (pl.ds(offsets.index(k), 1) for k in (offset, offset ^ bit))
        return 1.0 / (own[here, :] + other[there, :])

    def row_inverse(row):
        return jnp.broadcast_to(inverse(rows, row, row_bit, row_ref, row_other), (block, block)).T

    row_scale = {row: row_inverse(row) for row in rows}
    col_scale = {column: inverse(columns, column, col_bit, col_ref, col_other) for column in columns}

    def weights(row, column):
        index, k, c = grown[row, column]
        values = refs[index][pl.ds(k * block, block), pl.ds(c * block, block)]
        return (values * (row_scale[row] + col_scale[column])).astype(BF16)

    def audio_total():
        return sum(mm(weights(pick[0], column), text[column][...]) for column in columns)

    def text_total():
        return sum(mm(weights(row, pick[1]), audio[row][...], 0, 0) for row in rows)

    if pair_count is None:
        outs[0][...] = audio_total().astype(BF16)
        outs[1][...] = text_total().astype(BF16)
        return
    factor = scale_ref[0, 0] / (2.0 * pair_count)
    for side, (total, partner) in enumerate(((audio_total, text), (text_total, audio))):
        base_ref, unit_ref, inverse_ref = outs[3 * side : 3 * side + 3]
        values = sources[side][...].astype(F32)
        base_ref[...] = (total() - 2.0 * partner[0][...].astype(F32)) * factor
        scaled = lax.rsqrt(jnp.sum(values * values, axis=1, keepdims=True) + epsilon)
        unit_ref[...] = values * scaled
        inverse_ref[...] = jnp.broadcast_to(scaled, inverse_ref.shape)


def final_kernel(pair_count, sides, scale_ref, *refs):
    factor = scale_ref[0, 0] / (2.0 * pair_count)
    outs, stages, sems = refs[4 * sides : 5 * sides], refs[5 * sides : 6 * sides], refs[-1]
    copies = []
    for side in range(sides):
        base_ref, unit_ref, inverse_ref, other_ref = refs[4 * side : 4 * side + 4]
        total = base_ref[...] + other_ref[...].astype(F32) * factor
        unit = unit_ref[...]
        along = jnp.sum(unit * total, axis=1, keepdims=True)
        stages[side][...] = (total - unit * along) * inverse_ref[:, :1]
        copies.append(pltpu.make_async_copy(stages[side], outs[side], sems.at[side]))
        copies[-1].start()
    for copy in copies:
        copy.wait()


def local(frames, lengths, routes, w_first, b_first, w_second, captions, logit_scale):
    clips = lengths.shape[0]
    width = w_second.shape[1]
    group = lax.axis_size("blk")
    pair_count = clips * group * lax.axis_size("dp")
    bits = [1 << k for k in range(group.bit_length() - 1)]
    row_bit, col_bit = bits[1], bits[0]
    shared_bits = [bit for bit in bits if bit not in (row_bit, col_bit)]
    live_rows = min(routes.shape[1] * routes.shape[2], frames.shape[0])
    chunks = [live_rows // 2, live_rows // 4]
    chunks.append(live_rows - sum(chunks))
    scale = logit_scale.reshape(1, 1)
    block_low = jax.ShapeDtypeStruct((clips, width), BF16)
    block_full = jax.ShapeDtypeStruct((clips, width), F32)

    pooled, audio_low = pl.pallas_call(
        functools.partial(frames_kernel, chunks),
        out_shape=(block_full, block_low),
        in_specs=[HBM] * 5,
        out_specs=(VMEM, VMEM),
        scratch_shapes=[
            pltpu.VMEM((1, clips), lengths.dtype),
            pltpu.VMEM((1, width), F32),
            pltpu.VMEM(w_first.shape, BF16),
            pltpu.VMEM(w_second.shape, BF16),
            pltpu.VMEM((live_rows, frames.shape[1]), BF16),
            pltpu.SemaphoreType.DMA((len(chunks) + 4,)),
        ],
        compiler_params=PARAMS,
    )(
        *map(
            in_hbm,
            (lengths.reshape(1, clips), b_first.reshape(1, width), w_first, w_second, frames),
        )
    )
    def joined(arrays):
        return arrays[0] if len(arrays) == 1 else jnp.concatenate(arrays, axis=0)

    def gathered(block):
        arrays, offsets = [block], [0]
        for bit in shared_bits:
            arrays.append(swap(joined(arrays), bit))
            offsets += [k ^ bit for k in offsets]
        return arrays, offsets

    text, columns = gathered(captions)
    shared_text, _ = lax.optimization_barrier((text, audio_low))
    text += [swap(captions, col_bit), swap(joined(shared_text[1:]), col_bit)]
    columns += [k ^ col_bit for k in columns]
    audio, rows = gathered(audio_low)
    audio.append(swap(audio_low, row_bit))
    early_rows = rows + [row_bit]
    early_audio = list(audio)
    late_rows = [k ^ row_bit for k in rows[1:]]
    late_audio = [swap(joined(audio[1:-1]), row_bit)]

    def tile_shapes(row_offsets):
        count = len(row_offsets)
        return (
            jax.ShapeDtypeStruct((count * clips, len(columns) * clips), F32),
            jax.ShapeDtypeStruct((count, clips), F32),
            jax.ShapeDtypeStruct((len(columns), clips), F32),
        )

    early_grown, early_sum, col_sum, text_low = pl.pallas_call(
        functools.partial(early_tile_kernel, early_rows, columns, len(early_audio)),
        out_shape=(
            *tile_shapes(early_rows),
            jax.ShapeDtypeStruct((len(columns) * clips, width), BF16),
        ),
        in_specs=[SMEM] + [VMEM] * (len(early_audio) + len(text)),
        out_specs=[VMEM] * 4,
        compiler_params=PARAMS,
    )(scale, *early_audio, *text)
    late_grown, late_sum, col_sum = pl.pallas_call(
        functools.partial(late_tile_kernel, late_rows, columns),
        out_shape=tile_shapes(late_rows),
        in_specs=[SMEM] + [VMEM] * (len(late_audio) + 2),
        out_specs=[VMEM] * 3,
        compiler_params=PARAMS,
    )(scale, *late_audio, text_low, col_sum)
    row_sum = jnp.concatenate([early_sum, late_sum], axis=0)
    row_other, col_other = swap(row_sum, row_bit), swap(col_sum, col_bit)
    rows, audio = early_rows + late_rows, early_audio + late_audio
    operands = [early_grown, late_grown, row_sum, row_other, col_sum, col_other, *audio, text_low]

    def grads(pick, extra, pairs, kinds):
        return pl.pallas_call(
            functools.partial(grad_kernel, rows, columns, row_bit, col_bit, pick, pairs),
            out_shape=kinds,
            in_specs=[SMEM] + [VMEM] * (len(operands) + len(extra)),
            out_specs=[VMEM] * len(kinds),
            compiler_params=PARAMS,
        )(scale, *operands, *extra)

    audio_sent, text_sent = grads((row_bit, col_bit), [], None, [block_low] * 2)
    text_other, audio_other = swap(text_sent, col_bit), swap(audio_sent, row_bit)
    narrow = jax.ShapeDtypeStruct((clips, 128), F32)
    prepared = grads((0, 0), [pooled, captions], pair_count, [block_full, block_full, narrow] * 2)

    def final(*inputs):
        sides = len(inputs) // 4
        return pl.pallas_call(
            functools.partial(final_kernel, pair_count, sides),
            out_shape=[block_full] * sides,
            in_specs=[SMEM] + [VMEM] * len(inputs),
            out_specs=[HBM] * sides,
            scratch_shapes=[pltpu.VMEM((clips, width), F32)] * sides
            + [pltpu.SemaphoreType.DMA((sides,))],
            compiler_params=PARAMS,
        )(scale, *inputs)

    (audio_grad,) = final(*prepared[:3], audio_other)
    (text_grad,) = final(*prepared[3:], text_other)
    return audio_grad, text_grad


def solution(mesh):
    rows = P(("blk", "dp"))
    return jax.shard_map(
        local,
        mesh=mesh,
        in_specs=(rows, rows, rows, P(), P(), P(), rows, P()),
        out_specs=(rows, rows),
        check_vma=False,
    )
```

```python
import functools
import math

import jax
import jax.numpy as jnp
from jax import lax
from jax.experimental import pallas as pl
from jax.experimental.pallas import tpu as pltpu
from jax.sharding import PartitionSpec as P

epsilon = 1e-06
LOG2E = math.log2(math.e)
F32 = jnp.float32
BF16 = jnp.bfloat16
VMEM = pl.BlockSpec(memory_space=pltpu.VMEM)
SMEM = pl.BlockSpec(memory_space=pltpu.SMEM)
HBM = pl.BlockSpec(memory_space=pltpu.HBM)
PARAMS = pltpu.CompilerParams(vmem_limit_bytes=40 * 1024 * 1024)


def mm(left, right, left_dim=1, right_dim=0):
    return lax.dot_general(
        left, right, (((left_dim,), (right_dim,)), ((), ())), preferred_element_type=F32
    )


def in_hbm(array):
    return pltpu.with_memory_space_constraint(array, pltpu.HBM)


def swap(block, offset):
    count = lax.axis_size("blk")
    return lax.ppermute(block, "blk", [(i ^ offset, i) for i in range(count)])


def blocks_of(refs, offsets, block):
    parts = [ref.at[pl.ds(at, block)] for ref in refs for at in range(0, ref.shape[0], block)]
    return dict(zip(offsets, parts, strict=True))


def unit_low(values):
    return values * lax.rsqrt(jnp.sum(values * values, axis=1, keepdims=True) + epsilon)


def frames_kernel(chunks, *refs):
    lengths_hbm, bias_hbm, first_hbm, second_hbm, frames_hbm, pooled_ref, audio_ref = refs[:7]
    lengths_ref, bias_ref, first_ref, second_ref, held, sems = refs[7:]
    copies = []
    at = 0
    for k, rows in enumerate(chunks):
        part = pl.ds(at, rows)
        copies.append(pltpu.make_async_copy(frames_hbm.at[part], held.at[part], sems.at[k]))
        at += rows
    extra = []
    for k, pair in enumerate(
        [
            (first_hbm, first_ref),
            (lengths_hbm, lengths_ref),
            (bias_hbm, bias_ref),
            (second_hbm, second_ref),
        ]
    ):
        extra.append(pltpu.make_async_copy(*pair, sems.at[len(chunks) + k]))
    first_copy, lengths_copy, bias_copy, second_copy = extra
    for copy in [copies[0], first_copy, lengths_copy, bias_copy, second_copy, *copies[1:]]:
        copy.start()
    clips = lengths_ref.shape[1]
    lengths_copy.wait()
    lengths = lengths_ref[...].astype(F32)
    row_id = lax.broadcasted_iota(jnp.int32, (clips, clips), 0)
    col_id = lax.broadcasted_iota(jnp.int32, (clips, clips), 1)
    ends = jnp.sum(jnp.where(col_id <= row_id, lengths, 0.0), axis=1, keepdims=True)
    sizes = jnp.sum(jnp.where(col_id == row_id, lengths, 0.0), axis=1, keepdims=True)
    starts = ends - sizes
    live = jnp.sum(lengths_ref[...])
    bias_copy.wait()
    root = math.sqrt(2.0 / math.pi)

    def place_of(at, rows):
        place = lax.broadcasted_iota(jnp.int32, (clips, rows), 1).astype(F32) + float(at)
        return jnp.where((place >= starts) & (place < ends), 1.0, 0.0).astype(BF16)

    def pooled_chunk(at, rows, onehot):
        before = mm(held[pl.ds(at, rows), :], first_ref[...]) + bias_ref[...]
        half = before * 0.5
        inner = before * (root + (root * 0.044715) * (before * before))
        active = (half + half * jnp.tanh(inner)).astype(BF16)
        return mm(onehot, active)

    onehot = place_of(0, chunks[0])
    first_copy.wait()
    copies[0].wait()
    pooled_ref[...] = pooled_chunk(0, chunks[0], onehot)
    at = chunks[0]
    for k, rows in enumerate(chunks[1:], 1):
        copies[k].wait()

        @pl.when(live > at)
        def _():
            pooled_ref[...] += pooled_chunk(at, rows, place_of(at, rows))

        at += rows
    second_copy.wait()
    total = pooled_ref[...]
    high = total.astype(BF16)
    rest = (total - high.astype(F32)).astype(BF16)
    second = second_ref[...]
    both = mm(jnp.concatenate([high, rest], axis=0), second)
    pooled = (both[:clips] + both[clips:]) / sizes
    pooled_ref[...] = pooled
    audio_ref[...] = unit_low(pooled).astype(BF16)


def tile_kernel(rows, columns, audio_refs, text, col_sums, scale, grown_ref, row_ref, col_ref):
    block = row_ref.shape[1]
    audio = blocks_of(audio_refs, rows, block)
    for r, row in enumerate(rows):
        values = audio[row][...]
        partial = None
        downs = []
        whole = jnp.exp2(mm(values, text, 1, 1) * (scale * LOG2E))
        grown_ref[pl.ds(r * block, block), :] = whole
        for c in range(len(columns)):
            grown = whole[:, c * block : (c + 1) * block]
            downs.append(jnp.sum(grown, axis=0, keepdims=True))
            partial = grown if c == 0 else partial + grown
        col_sums = downs if col_sums is None else [x + y for x, y in zip(col_sums, downs, strict=True)]
        row_ref[pl.ds(r, 1), :] = jnp.sum(partial.T, axis=0, keepdims=True)
    for c in range(len(columns)):
        col_ref[pl.ds(c, 1), :] = col_sums[c]


def early_tile_kernel(rows, columns, audio_count, scale_ref, *refs):
    grown_ref, row_ref, col_ref, low_ref = refs[len(refs) - 4 :]
    block = row_ref.shape[1]
    raw = blocks_of(refs[audio_count : len(refs) - 4], columns, block)
    text = []
    for c, column in enumerate(columns):
        text.append(unit_low(raw[column][...].astype(F32)).astype(BF16))
        low_ref[pl.ds(c * block, block), :] = text[c]
    text = jnp.concatenate(text, axis=0)
    audio = refs[:audio_count]
    tile_kernel(rows, columns, audio, text, None, scale_ref[0, 0], grown_ref, row_ref, col_ref)


def late_tile_kernel(rows, columns, scale_ref, *refs):
    low_ref, sums_ref, early_ref, grown_ref, row_ref, col_ref = refs[len(refs) - 6 :]
    early = early_ref.shape[0]
    row_ref[pl.ds(0, early), :] = early_ref[...]
    row_ref = row_ref.at[pl.ds(early, len(rows))]
    block = row_ref.shape[1]
    text = low_ref[...]
    sums = [sums_ref[pl.ds(c, 1), :] for c in range(len(columns))]
    audio = refs[: len(refs) - 6]
    tile_kernel(rows, columns, audio, text, sums, scale_ref[0, 0], grown_ref, row_ref, col_ref)


def grad_kernel(rows, columns, row_bit, col_bit, pick, pair_count, scale_ref, *refs):
    block = refs[1].shape[1] // len(columns)
    count = len(rows)
    grown, near = {}, 0
    held = 0
    while held < count:
        for k in range(refs[near].shape[0] // block):
            for c, column in enumerate(columns):
                grown[rows[held], column] = (near, k, c)
            held += 1
        near += 1
    row_ref, row_other, col_ref, col_other = refs[near : near + 4]
    audio_refs, text_refs, at = [], [], near + 4
    for store, wanted in ((audio_refs, len(rows)), (text_refs, len(columns))):
        total = 0
        while total < wanted:
            store.append(refs[at])
            total += refs[at].shape[0] // block
            at += 1
    audio, text = blocks_of(audio_refs, rows, block), blocks_of(text_refs, columns, block)
    sources, outs = ([], refs[at:]) if pair_count is None else (refs[at : at + 2], refs[at + 2 :])

    def inverse(offsets, offset, bit, own, other):
        here, there = (pl.ds(offsets.index(k), 1) for k in (offset, offset ^ bit))
        return 1.0 / (own[here, :] + other[there, :])

    def row_inverse(row):
        return jnp.broadcast_to(inverse(rows, row, row_bit, row_ref, row_other), (block, block)).T

    row_scale = {row: row_inverse(row) for row in rows}
    col_scale = {column: inverse(columns, column, col_bit, col_ref, col_other) for column in columns}

    def weights(row, column):
        index, k, c = grown[row, column]
        values = refs[index][pl.ds(k * block, block), pl.ds(c * block, block)]
        return (values * (row_scale[row] + col_scale[column])).astype(BF16)

    def audio_total():
        row = jnp.concatenate([weights(pick[0], column) for column in columns], axis=1)
        return mm(row, jnp.concatenate([text[column][...] for column in columns], axis=0))

    def text_total():
        column = jnp.concatenate([weights(row, pick[1]) for row in rows], axis=0)
        return mm(column, jnp.concatenate([audio[row][...] for row in rows], axis=0), 0, 0)

    if pair_count is None:
        outs[0][...] = audio_total().astype(BF16)
        outs[1][...] = text_total().astype(BF16)
        return
    factor = scale_ref[0, 0] / (2.0 * pair_count)
    for side, (total, partner) in enumerate(((audio_total, text), (text_total, audio))):
        base_ref, unit_ref, inverse_ref = outs[3 * side : 3 * side + 3]
        values = sources[side][...].astype(F32)
        base_ref[...] = (total() - 2.0 * partner[0][...].astype(F32)) * factor
        scaled = lax.rsqrt(jnp.sum(values * values, axis=1, keepdims=True) + epsilon)
        unit_ref[...] = values * scaled
        inverse_ref[...] = jnp.broadcast_to(scaled, inverse_ref.shape)


def final_kernel(pair_count, sides, scale_ref, *refs):
    factor = scale_ref[0, 0] / (2.0 * pair_count)
    outs, stages, sems = refs[4 * sides : 5 * sides], refs[5 * sides : 6 * sides], refs[-1]
    copies = []
    for side in range(sides):
        base_ref, unit_ref, inverse_ref, other_ref = refs[4 * side : 4 * side + 4]
        total = base_ref[...] + other_ref[...].astype(F32) * factor
        unit = unit_ref[...]
        along = jnp.sum(unit * total, axis=1, keepdims=True)
        stages[side][...] = (total - unit * along) * inverse_ref[:, :1]
        copies.append(pltpu.make_async_copy(stages[side], outs[side], sems.at[side]))
        copies[-1].start()
    for copy in copies:
        copy.wait()


def local(frames, lengths, routes, w_first, b_first, w_second, captions, logit_scale):
    clips = lengths.shape[0]
    width = w_second.shape[1]
    group = lax.axis_size("blk")
    pair_count = clips * group * lax.axis_size("dp")
    bits = [1 << k for k in range(group.bit_length() - 1)]
    row_bit, col_bit = bits[1], bits[0]
    shared_bits = [bit for bit in bits if bit not in (row_bit, col_bit)]
    live_rows = min(routes.shape[1] * routes.shape[2], frames.shape[0])
    chunks = [live_rows // 2, live_rows // 4]
    chunks.append(live_rows - sum(chunks))
    scale = logit_scale.reshape(1, 1)
    block_low = jax.ShapeDtypeStruct((clips, width), BF16)
    block_full = jax.ShapeDtypeStruct((clips, width), F32)

    pooled, audio_low = pl.pallas_call(
        functools.partial(frames_kernel, chunks),
        out_shape=(block_full, block_low),
        in_specs=[HBM] * 5,
        out_specs=(VMEM, VMEM),
        scratch_shapes=[
            pltpu.VMEM((1, clips), lengths.dtype),
            pltpu.VMEM((1, width), F32),
            pltpu.VMEM(w_first.shape, BF16),
            pltpu.VMEM(w_second.shape, BF16),
            pltpu.VMEM((live_rows, frames.shape[1]), BF16),
            pltpu.SemaphoreType.DMA((len(chunks) + 4,)),
        ],
        compiler_params=PARAMS,
    )(
        *map(
            in_hbm,
            (lengths.reshape(1, clips), b_first.reshape(1, width), w_first, w_second, frames),
        )
    )
    def joined(arrays):
        return arrays[0] if len(arrays) == 1 else jnp.concatenate(arrays, axis=0)

    def gathered(block):
        arrays, offsets = [block], [0]
        for bit in shared_bits:
            arrays.append(swap(joined(arrays), bit))
            offsets += [k ^ bit for k in offsets]
        return arrays, offsets

    text, columns = gathered(captions)
    shared_text, _ = lax.optimization_barrier((text, audio_low))
    text += [swap(captions, col_bit), swap(joined(shared_text[1:]), col_bit)]
    columns += [k ^ col_bit for k in columns]
    audio, rows = gathered(audio_low)
    audio.append(swap(audio_low, row_bit))
    early_rows = rows + [row_bit]
    early_audio = list(audio)
    late_rows = [k ^ row_bit for k in rows[1:]]
    late_audio = [swap(joined(audio[1:-1]), row_bit)]

    def tile_shapes(row_offsets):
        count = len(row_offsets)
        return (
            jax.ShapeDtypeStruct((count * clips, len(columns) * clips), F32),
            jax.ShapeDtypeStruct((count, clips), F32),
            jax.ShapeDtypeStruct((len(columns), clips), F32),
        )

    early_grown, early_sum, col_sum, text_low = pl.pallas_call(
        functools.partial(early_tile_kernel, early_rows, columns, len(early_audio)),
        out_shape=(
            *tile_shapes(early_rows),
            jax.ShapeDtypeStruct((len(columns) * clips, width), BF16),
        ),
        in_specs=[SMEM] + [VMEM] * (len(early_audio) + len(text)),
        out_specs=[VMEM] * 4,
        compiler_params=PARAMS,
    )(scale, *early_audio, *text)
    late_grown, late_sum, col_sum = pl.pallas_call(
        functools.partial(late_tile_kernel, late_rows, columns),
        out_shape=(
            tile_shapes(late_rows)[0],
            jax.ShapeDtypeStruct((len(early_rows + late_rows), clips), F32),
            tile_shapes(late_rows)[2],
        ),
        in_specs=[SMEM] + [VMEM] * (len(late_audio) + 3),
        out_specs=[VMEM] * 3,
        compiler_params=PARAMS,
    )(scale, *late_audio, text_low, col_sum, early_sum)
    row_sum = late_sum
    row_other, col_other = swap(row_sum, row_bit), swap(col_sum, col_bit)
    rows, audio = early_rows + late_rows, early_audio + late_audio
    operands = [early_grown, late_grown, row_sum, row_other, col_sum, col_other, *audio, text_low]

    def grads(pick, extra, pairs, kinds):
        return pl.pallas_call(
            functools.partial(grad_kernel, rows, columns, row_bit, col_bit, pick, pairs),
            out_shape=kinds,
            in_specs=[SMEM] + [VMEM] * (len(operands) + len(extra)),
            out_specs=[VMEM] * len(kinds),
            compiler_params=PARAMS,
        )(scale, *operands, *extra)

    audio_sent, text_sent = grads((row_bit, col_bit), [], None, [block_low] * 2)
    text_other, audio_other = swap(text_sent, col_bit), swap(audio_sent, row_bit)
    narrow = jax.ShapeDtypeStruct((clips, 128), F32)
    prepared = grads((0, 0), [pooled, captions], pair_count, [block_full, block_full, narrow] * 2)

    def final(*inputs):
        sides = len(inputs) // 4
        return pl.pallas_call(
            functools.partial(final_kernel, pair_count, sides),
            out_shape=[block_full] * sides,
            in_specs=[SMEM] + [VMEM] * len(inputs),
            out_specs=[HBM] * sides,
            scratch_shapes=[pltpu.VMEM((clips, width), F32)] * sides
            + [pltpu.SemaphoreType.DMA((sides,))],
            compiler_params=PARAMS,
        )(scale, *inputs)

    (audio_grad,) = final(*prepared[:3], audio_other)
    (text_grad,) = final(*prepared[3:], text_other)
    return audio_grad, text_grad


def solution(mesh):
    rows = P(("blk", "dp"))
    return jax.shard_map(
        local,
        mesh=mesh,
        in_specs=(rows, rows, rows, P(), P(), P(), rows, P()),
        out_specs=(rows, rows),
        check_vma=False,
    )
```
